32 devices in a mesh: groups: 2 (over x), vocab: 16 (over z, y, core).
Axes of the slice: x: 2, y: 2, z: 4, core: 2. Of those that a mesh axis runs over, the one named last changes fastest.
Arguments:
- backbone_feature_matrix: bfloat16 [256, 5120], P(('groups', 'vocab')), parts along dimension 0, may hold values from -100 to 100, as said below
- closing_rmsnorm_multiplier: float32 [10240], P('groups'), parts along dimension 0, may hold values from 0.5 to 1.5
- output_vocab_matrix: bfloat16 [10240, 20480], P('groups', 'vocab'), parts along dimension 0, may hold values from -100 to 100, as said below
- softness_divisor: float32 [2], P('groups'), parts along dimension 0, may hold values from 0.8 to 1.6
- correct_label_ids: int32 [256], P(('groups', 'vocab')), parts along dimension 0, may hold values from 0 to 20479
- included_place_flags: int32 [256], P(('groups', 'vocab')), parts along dimension 0, may hold values from 0 to 1, as said below
Outputs:
- grad_hidden: bfloat16 [256, 5120], P(('groups', 'vocab')), parts along dimension 0
- grad_gain: float32 [10240], P('groups'), parts along dimension 0
- grad_temp: float32 [2], P('groups'), parts along dimension 0
- loss_mean: float32 [2], P('groups'), parts along dimension 0
The draws below stay inside these ranges and needn't reach their ends.
There are 2 independent parts, one for each index of `groups`. The reference program is written for one: setup_inputs(seed, part) draws one part's arguments, and reference() takes and returns one part's arrays. A program takes and returns all parts, laid end to end along the dimension named above; each array names one. Nothing has to cross between parts.
Inputs may be any that keep to these rules, and one draw needn't show every extreme that they name: `backbone_feature_matrix`: activations of one member. `output_vocab_matrix`: head weights of one member. `included_place_flags`: in the member with index 1 every entry is 0.
All inputs are finite; a program needn't handle non-finite values.
Results may differ from the reference program's by a relative error of at most 0.0052.
Values may be sent and summed in bfloat16 or wider, within the bound.
No kernel may reach another device: no remote copies, remote signals or barrier semaphores. Data moves between devices by JAX's collectives and lax.ppermute only.
A program may use at most 128 MiB of HBM per device.

```python
import math
import jax
import jax.numpy as jnp
import numpy as np
from jax import lax

D = 5120
TOKENS = 128
VOCAB = 20480


def shared_draw(key):
    base_rows = jax.random.normal(jax.random.fold_in(key, 1), (TOKENS, D), jnp.float32)
    feature_scale = jnp.exp(jax.random.uniform(jax.random.fold_in(key, 3), (D,), jnp.float32) * math.log(10.0))
    return (base_rows, feature_scale)


def directions(key):
    base_rows, feature_scale = shared_draw(key)
    return base_rows * feature_scale[None, :]


def draw_backbone_feature_matrix(key, part):
    own_key = jax.random.fold_in(key, 11)
    aligned = directions(key)
    spread = math.log(10.0)
    row_scale = 0.1 * jnp.exp(jax.random.uniform(own_key, (TOKENS, 1), jnp.float32) * spread)
    return (aligned * row_scale).astype(jnp.bfloat16)


def draw_output_vocab_matrix(key, part):
    own_key = jax.random.fold_in(key, 12)
    weight = jax.random.normal(own_key, (D, VOCAB), jnp.float32) * (5.0 / math.sqrt(D))
    return weight.astype(jnp.bfloat16)


def draw_included_place_flags(key, part):
    key = jax.random.fold_in(key, 13)
    levels = jax.random.randint(key, (TOKENS,), 0, 4)
    kept = (levels != 0).astype(jnp.int32)
    return jnp.where(part == 1, jnp.zeros_like(kept), kept)


def touch_ends(array, key, low, high):
    longest = array.shape.index(max(array.shape))
    spots = []
    for shift in (0, 1):
        where = [jax.random.randint(jax.random.fold_in(key, axis), (), 0, length) for axis, length in enumerate(array.shape)]
        where[longest] = (where[longest] + shift) % array.shape[longest]
        spots.append(tuple(where))
    return array.at[spots[0]].set(low).at[spots[1]].set(high)


def rank_bounds(number_of, skew):
    weights = [(1 << 20) // math.isqrt(grade ** skew) + 1 for grade in range(1, number_of + 1)]
    scale = 1 + sum(weights) // (1 << 30)
    return np.cumsum(np.array([max(1, weight // scale) for weight in weights]))


def skewed_ids(rng, dims, count, lean):
    listing = rank_bounds(count, lean)
    pick = jax.random.randint(jax.random.fold_in(rng, 1), dims, 0, int(listing[count - 1]))
    grade = jnp.searchsorted(jnp.asarray(listing, jnp.int32), pick, side="right")
    return jax.random.permutation(jax.random.fold_in(rng, 2), count)[grade].astype(jnp.int32)


def setup_inputs(seed: int = 0, part: int = 0) -> dict:
    keys = jax.random.split(jax.random.key(seed), 7)
    part_splits = jax.random.split(jax.random.fold_in(keys[6], part), 7)
    backbone_feature_matrix = draw_backbone_feature_matrix(jax.random.fold_in(jax.random.fold_in(keys[6], part), 71), part)
    closing_rmsnorm_multiplier = jnp.clip(1.0 + 0.1 * jax.random.normal(part_splits[1], (D,), jnp.float32), 0.5, 1.5)
    output_vocab_matrix = draw_output_vocab_matrix(jax.random.fold_in(jax.random.fold_in(keys[6], part), 71), part)
    softness_divisor = jnp.clip(jnp.exp(jax.random.uniform(part_splits[3], (1,), jnp.float32, math.log(0.8), math.log(1.6))), 0.8, 1.6)
    correct_label_ids = touch_ends(skewed_ids(part_splits[4], (TOKENS,), VOCAB, 2), jax.random.fold_in(part_splits[4], 3), 0, VOCAB - 1).astype(jnp.int32)
    included_place_flags = draw_included_place_flags(jax.random.fold_in(jax.random.fold_in(keys[6], part), 71), part)
    return {"backbone_feature_matrix": backbone_feature_matrix, "closing_rmsnorm_multiplier": closing_rmsnorm_multiplier, "output_vocab_matrix": output_vocab_matrix, "softness_divisor": softness_divisor, "correct_label_ids": correct_label_ids, "included_place_flags": included_place_flags}


epsilon = 1e-06

def reference(backbone_feature_matrix, closing_rmsnorm_multiplier, output_vocab_matrix, softness_divisor, correct_label_ids, included_place_flags):
    raw_rows = backbone_feature_matrix.astype(jnp.float32)
    inv_rms = lax.rsqrt(lax.optimization_barrier(jnp.mean(raw_rows * raw_rows, axis=1, keepdims=True)) + epsilon)
    unit_rows = raw_rows * inv_rms
    normed = (unit_rows * closing_rmsnorm_multiplier[None, :]).astype(jnp.bfloat16)
    logits = jnp.dot(normed, output_vocab_matrix, preferred_element_type=jnp.float32)
    divisor_tally = softness_divisor[0]
    scaled = logits / divisor_tally
    peak = lax.optimization_barrier(jnp.max(scaled, axis=1))
    exp_terms = jnp.exp(scaled - peak[:, None])
    totals = lax.optimization_barrier(jnp.sum(exp_terms, axis=1))
    moments = lax.optimization_barrier(jnp.sum(exp_terms * scaled, axis=1))
    onehot = (lax.broadcasted_iota(jnp.int32, scaled.shape, 1) == correct_label_ids[:, None]).astype(jnp.float32)
    target_z = lax.optimization_barrier(jnp.sum(onehot * scaled, axis=1))
    mask_f = included_place_flags.astype(jnp.float32)
    counted = jnp.maximum(jnp.sum(mask_f), 1.0)
    loss_mean = jnp.sum(mask_f * (peak + jnp.log(totals) - target_z)) / counted
    grad_temp = -jnp.sum(mask_f * (moments / totals - target_z)) / (counted * divisor_tally)
    factor = mask_f * (TOKENS / counted) / divisor_tally
    logit_grad = (factor[:, None] * (exp_terms / totals[:, None] - onehot)).astype(jnp.bfloat16)
    normed_grad = lax.dot_general(logit_grad, output_vocab_matrix, (((1,), (1,)), ((), ())), preferred_element_type=jnp.float32)
    unit_scale_gradient = normed_grad * closing_rmsnorm_multiplier[None, :]
    inner_dot = lax.optimization_barrier(jnp.sum(unit_scale_gradient * unit_rows, axis=1, keepdims=True))
    grad_hidden = (inv_rms * (unit_scale_gradient - unit_rows * inner_dot / D)).astype(jnp.bfloat16)
    grad_gain = lax.optimization_barrier(jnp.sum(normed_grad * unit_rows, axis=0))
    return (grad_hidden, grad_gain, grad_temp[None], loss_mean[None])
```

```python
import jax
import jax.numpy as jnp
from jax import lax
from jax.sharding import PartitionSpec as P

epsilon = 1e-06
f32 = jnp.float32
bf16 = jnp.bfloat16
DIGIT = 128


def cat(*parts):
    return jnp.concatenate(parts, 0)


def bits_of(count):
    return [1 << b for b in range(count.bit_length() - 1)]


class Links:
    def __init__(self, count):
        self.count = count

    def swap(self, value, m):
        return lax.ppermute(value, "vocab", [(i, i ^ m) for i in range(self.count)])

    def gather(self, own):
        swap = self.swap
        if self.count == 16:
            far, diagonal, near, side = swap(own, 8), swap(own, 12), swap(own, 4), swap(own, 2)
            column = cat(far, diagonal, near)
            across = swap(column, 2)
            twin = swap(cat(own, side, column), 1)
            twin_across = swap(across, 1)
            return cat(own, side, column, across, twin, twin_across)
        blocks = own
        for m in reversed(bits_of(self.count)):
            blocks = cat(blocks, swap(blocks, m))
        return blocks

    def codes(self):
        if self.count == 16:
            first = [0, 2, 8, 12, 4, 10, 14, 6]
            return first + [c ^ 1 for c in first]
        codes = [0]
        for m in reversed(bits_of(self.count)):
            codes = codes + [c ^ m for c in codes]
        return codes

    def scatter(self, blocks):
        swap = self.swap
        if self.count == 16:
            b = blocks.shape[0] // 16
            g = blocks[: 8 * b] + swap(blocks[8 * b :].astype(bf16), 1).astype(f32)
            g0, g2, g8, g12, g4, g10, g14, g6 = [g[k * b : (k + 1) * b] for k in range(8)]
            s12 = swap(g14.astype(bf16), 2).astype(f32)
            s84 = swap(cat(g10, g6).astype(bf16), 2).astype(f32)
            s0 = swap(g2.astype(bf16), 2).astype(f32)
            w8 = swap((g12 + s12).astype(bf16), 4).astype(f32)
            z8 = swap((g8 + s84[:b] + w8).astype(bf16), 8).astype(f32)
            z4 = swap((g4 + s84[b:]).astype(bf16), 4).astype(f32)
            return g0 + s0 + z4 + z8
        for m in bits_of(self.count):
            half = blocks.shape[0] // 2
            blocks = blocks[:half] + swap(blocks[half:].astype(bf16), m).astype(f32)
        return blocks

    def total(self, value):
        for m in bits_of(self.count):
            value = value + self.swap(value, m)
        return value


def merge(a, b):
    first = a[0] >= b[0]
    high, low = jnp.where(first, a, b), jnp.where(first, b, a)
    fade = jnp.exp(low[0] - high[0])
    return jnp.stack(
        [high[0], high[1] + low[1] * fade, high[2] + low[2] * fade, a[3] + b[3]]
    )


def on_device(
    backbone_feature_matrix,
    closing_rmsnorm_multiplier,
    output_vocab_matrix,
    softness_divisor,
    correct_label_ids,
    included_place_flags,
):
    count = lax.axis_size("vocab")
    links = Links(count)
    codes = links.codes()
    me = lax.axis_index("vocab")
    own_count, width = backbone_feature_matrix.shape
    token_count = own_count * count
    slab_width = output_vocab_matrix.shape[1]
    gain = closing_rmsnorm_multiplier[None, :]

    raw_rows = backbone_feature_matrix.astype(f32)
    inv_rms = lax.rsqrt(jnp.mean(raw_rows * raw_rows, axis=1, keepdims=True) + epsilon)
    own_units = raw_rows * inv_rms
    own_normed = (own_units * gain).astype(bf16)
    ids = correct_label_ids[:, None]
    lane = lax.broadcasted_iota(jnp.int32, (own_count, 128), 1)
    notes = jnp.where(
        lane == 0,
        ids % DIGIT,
        jnp.where(
            lane == 1,
            ids // DIGIT % DIGIT,
            jnp.where(
                lane == 2,
                ids // (DIGIT * DIGIT),
                jnp.where(lane == 3, included_place_flags[:, None], 0),
            ),
        ),
    ).astype(bf16)
    gathered = links.gather(jnp.concatenate([own_normed, notes], 1))
    normed = gathered[:, :width]
    noted = gathered[:, width:].astype(f32)
    targets = (
        noted[:, 0] + DIGIT * noted[:, 1] + DIGIT * DIGIT * noted[:, 2]
    ).astype(jnp.int32)
    mask_f = noted[:, 3]

    logits = jnp.dot(normed, output_vocab_matrix, preferred_element_type=f32)
    divisor_tally = softness_divisor[0]
    scaled = logits / divisor_tally
    owned = (
        lax.broadcasted_iota(jnp.int32, scaled.shape, 1) + me * slab_width
        == targets[:, None]
    )
    local_peak = jnp.max(scaled, axis=1)
    local_exp = jnp.exp(scaled - local_peak[:, None])
    local = jnp.stack(
        [
            local_peak,
            jnp.sum(local_exp, axis=1),
            jnp.sum(local_exp * scaled, axis=1),
            jnp.sum(jnp.where(owned, scaled, 0.0), axis=1),
            mask_f,
        ]
    )

    owners = me ^ jnp.array(codes, jnp.int32)
    place = lax.broadcasted_iota(jnp.int32, (count, count), 0) == owners[None, :]

    def to_shared(x):
        x = x.reshape(-1, 1, count, own_count)
        return jnp.sum(jnp.where(place[None, :, :, None], x, 0.0), 2).reshape(-1, token_count)

    def to_local(x):
        x = x.reshape(-1, count, 1, own_count)
        return jnp.sum(jnp.where(place[None, :, :, None], x, 0.0), 1).reshape(-1, token_count)

    shared = to_shared(local)
    shared_mask = shared[4]
    stats = shared[:4]
    if count == 16:
        near, far, diagonal = (links.swap(stats, m) for m in (4, 8, 12))
        stats = merge(merge(stats, near), merge(far, diagonal))
        stats = merge(stats, links.swap(stats, 2))
        stats = merge(stats, links.swap(stats, 1))
    else:
        for m in reversed(bits_of(count)):
            stats = merge(stats, links.swap(stats, m))
    peak, totals, moments, target_z = stats
    counted = jnp.maximum(jnp.sum(shared_mask), 1.0)
    loss_mean = jnp.sum(shared_mask * (peak + jnp.log(totals) - target_z)) / counted
    grad_temp = -jnp.sum(shared_mask * (moments / totals - target_z)) / (counted * divisor_tally)

    peak, totals = to_local(jnp.stack([peak, totals]))
    factor = mask_f * (token_count / counted) / divisor_tally
    exp_terms = jnp.exp(scaled - peak[:, None])
    logit_grad = (
        factor[:, None] * (exp_terms / totals[:, None] - owned.astype(f32))
    ).astype(bf16)
    slab_grad = lax.dot_general(
        logit_grad,
        output_vocab_matrix,
        (((1,), (1,)), ((), ())),
        preferred_element_type=f32,
    )
    grad_gain = links.total(
        jnp.sum(slab_grad * normed.astype(f32), axis=0) / closing_rmsnorm_multiplier
    )
    normed_grad = links.scatter(slab_grad)
    unit_grad = normed_grad * gain
    inner_dot = jnp.sum(unit_grad * own_units, axis=1, keepdims=True)
    grad_hidden = (inv_rms * (unit_grad - own_units * inner_dot / width)).astype(bf16)
    return (grad_hidden, grad_gain, grad_temp[None], loss_mean[None])


def solution(mesh):
    in_specs = (
        P(("groups", "vocab"), None),
        P("groups"),
        P("groups", "vocab"),
        P("groups"),
        P(("groups", "vocab")),
        P(("groups", "vocab")),
    )
    out_specs = (P(("groups", "vocab"), None), P("groups"), P("groups"), P("groups"))
    return jax.shard_map(
        on_device, mesh=mesh, in_specs=in_specs, out_specs=out_specs, check_vma=False
    )
```

```python
import functools

import jax
import jax.numpy as jnp
from jax import lax
from jax.experimental import pallas as pl
from jax.experimental.pallas import tpu as pltpu
from jax.sharding import PartitionSpec as P

epsilon = 1e-06
f32 = jnp.float32
bf16 = jnp.bfloat16
LANES = 128
DIGIT_BITS = 7
DIGIT = 1 << DIGIT_BITS
MIB = 1 << 20
STACK_FLOPS = 20 * 10**9


def cat(*parts):
    return jnp.concatenate(parts, 0)


def bits_of(count):
    return [1 << b for b in range(count.bit_length() - 1)]


class Links:
    def __init__(self, count):
        self.count = count

    def swap(self, value, m):
        return lax.ppermute(value, "vocab", [(i, i ^ m) for i in range(self.count)])

    def gather(self, own):
        swap = self.swap
        if self.count == 16:
            far, diagonal, near, side = swap(own, 8), swap(own, 12), swap(own, 4), swap(own, 2)
            column = stack_blocks(far, diagonal, near)
            across = swap(column, 2)
            twin = swap(cat(own, side, column), 1)
            twin_across = swap(across, 1)
            return cat(own, side, column, across, twin, twin_across)
        blocks = own
        for m in reversed(bits_of(self.count)):
            blocks = cat(blocks, swap(blocks, m))
        return blocks

    def codes(self):
        if self.count == 16:
            first = [0, 2, 8, 12, 4, 10, 14, 6]
            return first + [c ^ 1 for c in first]
        codes = [0]
        for m in reversed(bits_of(self.count)):
            codes = codes + [c ^ m for c in codes]
        return codes

    def gather_small(self, own):
        swap = self.swap
        if self.count == 16:
            column = cat(own, swap(own, 4), swap(own, 8), swap(own, 12))
            return cat(column, swap(column, 1), swap(column, 2), swap(column, 3))
        tiles = own
        for m in bits_of(self.count):
            tiles = cat(tiles, swap(tiles, m))
        return tiles

    def small_place(self, code):
        if self.count == 16:
            return (code & 3) * 4 + (code >> 2)
        return code


def spec(space=pltpu.VMEM):
    return pl.BlockSpec(memory_space=space)


SMEM, VMEM, HBM = spec(pltpu.SMEM), spec(), spec(pltpu.HBM)


def call(kernel, outs, ins, scratch=(), flops=0, moved=0, limit=24):
    return pl.pallas_call(
        kernel,
        out_shape=outs,
        in_specs=ins,
        out_specs=jax.tree.map(lambda _: spec(), outs),
        scratch_shapes=list(scratch),
        compiler_params=pltpu.CompilerParams(vmem_limit_bytes=limit * MIB),
        cost_estimate=pl.CostEstimate(flops=flops, bytes_accessed=moved, transcendentals=0),
    )


def shaped(shape, dtype):
    return jax.ShapeDtypeStruct(shape, dtype)


def norm_kernel(ids_hbm, flags_hbm, rows_hbm, gain_hbm, out_ref, ids, flags, rows, gain, sems):
    copies = [
        pltpu.make_async_copy(src, dst, sems.at[k])
        for k, (src, dst) in enumerate(
            [(rows_hbm, rows), (gain_hbm, gain), (ids_hbm, ids), (flags_hbm, flags)]
        )
    ]
    for copy in copies:
        copy.start()
    for copy in copies:
        copy.wait()
    raw = rows[...].astype(f32)
    own_count, width = raw.shape
    inv_rms = lax.rsqrt(jnp.mean(raw * raw, axis=1, keepdims=True) + epsilon)
    out_ref[:, :width] = (raw * inv_rms * gain[...]).astype(bf16)
    row = lax.broadcasted_iota(jnp.int32, (own_count, LANES), 0)
    lane = lax.broadcasted_iota(jnp.int32, (own_count, LANES), 1)
    notes = jnp.zeros((own_count, LANES), jnp.int32)
    for r in range(own_count):
        label = ids[r]
        digits = (
            label & (DIGIT - 1),
            (label >> DIGIT_BITS) & (DIGIT - 1),
            label >> (2 * DIGIT_BITS),
            flags[r],
        )
        for k, digit in enumerate(digits):
            notes = jnp.where((row == r) & (lane == k), digit, notes)
    out_ref[:, width:] = notes.astype(f32).astype(bf16)


def stack_kernel(*refs):
    ins, out_ref = refs[:-1], refs[-1]
    out_ref[...] = cat(*[ref[...].astype(f32) for ref in ins]).astype(out_ref.dtype)


def stack_blocks(*blocks):
    rows, width = blocks[0].shape
    return call(
        stack_kernel,
        shaped((len(blocks) * rows, width), bf16),
        [VMEM] * len(blocks),
        flops=STACK_FLOPS,
    )(*blocks)


def fold(row):
    c = row.shape[1] // 8
    return cat(*[row[:, k * c : (k + 1) * c] for k in range(8)])


def two_parts(value):
    high = value.astype(bf16).astype(f32)
    return jnp.concatenate([high, value - high], 1)


def one_value(parts):
    c = parts.shape[1] // 2
    return parts[:, :c] + parts[:, c:]


def read_notes(noted):
    label = noted[:, 0:1] + DIGIT * noted[:, 1:2] + DIGIT * DIGIT * noted[:, 2:3]
    return label.astype(jnp.int32), noted[:, 3:4]


def owned_mask(labels, me, slab_width):
    column = lax.broadcasted_iota(jnp.int32, (labels.shape[0], slab_width), 1)
    return column == labels - me * slab_width


def logits_kernel(codes, divisor_ref, rows_ref, head_ref, scaled_ref, stats_ref, blocks):
    me = lax.axis_index("vocab")
    width, slab_width = head_ref.shape
    token_count = rows_ref.shape[0]
    own_count = token_count // len(codes)
    scaled_ref[...] = (
        jnp.dot(rows_ref[:, :width], head_ref[...], preferred_element_type=f32) / divisor_ref[0]
    )
    chunk = 128
    for c in range(token_count // chunk):
        band = slice(c * chunk, (c + 1) * chunk)
        scaled = scaled_ref[band, :]
        labels, mask_f = read_notes(rows_ref[band, width:].astype(f32))
        owned = owned_mask(labels, me, slab_width)
        peak = jnp.max(scaled, axis=1, keepdims=True)
        exp_terms = jnp.exp(scaled - peak)
        columns = (
            peak,
            jnp.sum(exp_terms, axis=1, keepdims=True),
            jnp.sum(exp_terms * scaled, axis=1, keepdims=True),
            jnp.sum(jnp.where(owned, scaled, 0.0), axis=1, keepdims=True),
            mask_f,
        )
        lane = lax.broadcasted_iota(jnp.int32, (chunk, LANES), 1)
        tile = jnp.zeros((chunk, LANES), f32)
        for k, column in enumerate(columns):
            tile = jnp.where(lane == k, column, tile)
        for b in range(chunk // own_count):
            owner = me ^ codes[c * (chunk // own_count) + b]
            blocks[owner] = tile[b * own_count : (b + 1) * own_count]
    for c in range(token_count // chunk):
        per = chunk // own_count
        shared = blocks[c * per : (c + 1) * per].reshape(chunk, LANES)
        stats_ref[:, c * chunk : (c + 1) * chunk] = shared.T[:8]


def slab_kernel(
    codes,
    place,
    divisor_ref,
    tiles_ref,
    rows_ref,
    scaled_ref,
    head_ref,
    gain_ref,
    scalars_ref,
    parts_ref,
    kept_ref,
    sent_ref,
    turned,
    coefs,
    turned_coefs,
    gain_grad,
):
    me = lax.axis_index("vocab")
    count = len(codes)
    width, slab_width = head_ref.shape
    token_count = rows_ref.shape[0]
    own_count = token_count // count
    half = token_count // 2

    def tile(device):
        start = place(device ^ me) * 8
        return tiles_ref[pl.ds(pl.multiple_of(start, 8), 8), :]

    peak = tile(0)[0:1]
    for j in range(1, count):
        peak = jnp.maximum(peak, tile(j)[0:1])
    totals = moments = target_z = jnp.zeros_like(peak)
    for j in range(count):
        t = tile(j)
        fade = jnp.exp(t[0:1] - peak)
        totals += t[1:2] * fade
        moments += t[2:3] * fade
        target_z += t[3:4]
    mask_f = tile(me)[4:5]
    divisor = divisor_ref[0]
    counted = jnp.maximum(jnp.sum(mask_f, axis=1, keepdims=True), 1.0)
    loss = jnp.sum(mask_f * (peak + jnp.log(totals) - target_z), axis=1, keepdims=True) / counted
    temp = -jnp.sum(mask_f * (moments / totals - target_z), axis=1, keepdims=True) / (
        counted * divisor
    )
    lane = lax.broadcasted_iota(jnp.int32, (8, LANES), 1)
    scalars_ref[...] = jnp.where(lane == 0, loss, jnp.where(lane == 1, temp, 0.0))

    factor = mask_f * (token_count / counted) / divisor
    terms = cat(peak, totals, factor, jnp.zeros((LANES - 3, token_count), f32))
    turned[...] = terms.T.reshape(count, own_count, LANES)
    chunk = 64
    per = chunk // own_count
    for c in range(token_count // chunk):
        band = slice(c * chunk, (c + 1) * chunk)
        w = cat(*[turned[me ^ code] for code in codes[c * per : (c + 1) * per]])
        labels, _ = read_notes(rows_ref[band, width:].astype(f32))
        owned = owned_mask(labels, me, slab_width).astype(f32)
        shares = jnp.exp(scaled_ref[band, :] - w[:, 0:1]) / w[:, 1:2]
        coefs[band, :] = w[:, 2:3] * (shares - owned)
    turned_coefs[...] = coefs[...].T.astype(bf16)
    step = width // 2

    @pl.loop(0, width // step)
    def _(n):
        here = pl.ds(pl.multiple_of(n * step, step), step)
        out = jnp.dot(head_ref[here, :], turned_coefs[...], preferred_element_type=f32).T
        kept_ref[:, here] = out[:half]
        sent_ref[:half, here] = out[half:].astype(bf16)
        gain_grad[:, here] = (
            jnp.sum(out * rows_ref[:, here].astype(f32), axis=0, keepdims=True) / gain_ref[:, here]
        )

    parts = two_parts(fold(gain_grad[...])).astype(bf16)
    parts_ref[...] = parts
    sent_ref[half:, : parts.shape[1]] = parts
    sent_ref[half:, parts.shape[1] :] = jnp.zeros((8, width - parts.shape[1]), bf16)


def with_parts(block, gain_sum):
    return jnp.concatenate([block, two_parts(gain_sum)], 1).astype(bf16)


def pair_kernel(order, kept_ref, twin_ref, parts_ref, kept_out, more_out, first_out):
    count = len(order[0]) + len(order[1]) + 1
    half, width = kept_ref.shape
    own_count = half // count
    blocks = [None] * count
    for k in range(count // 2):
        band = slice(2 * k * own_count, 2 * (k + 1) * own_count)
        total = kept_ref[band, :] + twin_ref[band, :].astype(f32)
        blocks[2 * k], blocks[2 * k + 1] = total[:own_count], total[own_count:]
    twin_parts = twin_ref[half:, : parts_ref.shape[1]].astype(f32)
    gain_sum = one_value(parts_ref[...].astype(f32)) + one_value(twin_parts)
    kept_out[...] = cat(*[blocks[k] for k in order[0]])
    more_out[...] = cat(*[blocks[k] for k in order[1]]).astype(bf16)
    first_out[...] = with_parts(blocks[order[2]], gain_sum)


def hop_kernel(at, sent_ref, got_ref, kept_ref, *refs):
    more, out_ref = refs[:-1], refs[-1]
    own_count = sent_ref.shape[0]
    width = kept_ref.shape[1]
    block = kept_ref[at * own_count : (at + 1) * own_count, :] + got_ref[:, :width].astype(f32)
    for ref in more:
        block = block + ref[...].astype(f32)[:own_count]
    gain_sum = one_value(sent_ref[:, width:].astype(f32)) + one_value(
        got_ref[:, width:].astype(f32)
    )
    out_ref[...] = with_parts(block, gain_sum)


def hidden_kernel(places, rows_ref, gain_ref, kept_ref, sent_ref, got_ref, *refs):
    more, (out_ref, gain_out) = refs[:-2], refs[-2:]
    rows = rows_ref[...].astype(f32)
    own_count, width = rows.shape
    inv_rms = lax.rsqrt(jnp.mean(rows * rows, axis=1, keepdims=True) + epsilon)
    units = rows * inv_rms
    grad = kept_ref[:own_count, :] + got_ref[:, :width].astype(f32)
    for ref, at in zip(more, places):
        grad = grad + ref[...].astype(f32)[at * own_count : (at + 1) * own_count]
    grad = grad * gain_ref[...]
    inner_dot = jnp.sum(grad * units, axis=1, keepdims=True)
    out_ref[...] = (inv_rms * (grad - units * inner_dot / width)).astype(bf16)
    gain_sum = one_value(sent_ref[:, width:].astype(f32)) + one_value(
        got_ref[:, width:].astype(f32)
    )
    c = width // 8
    for k in range(8):
        gain_out[:, k * c : (k + 1) * c] = gain_sum[k : k + 1, :]


def on_device(
    backbone_feature_matrix,
    closing_rmsnorm_multiplier,
    output_vocab_matrix,
    softness_divisor,
    correct_label_ids,
    included_place_flags,
):
    count = lax.axis_size("vocab")
    links = Links(count)
    swap = links.swap
    codes = links.codes()
    own_count, width = backbone_feature_matrix.shape
    token_count = own_count * count
    half = token_count // 2
    slab_width = output_vocab_matrix.shape[1]
    gain = closing_rmsnorm_multiplier[None, :]
    head_bytes = 2 * width * slab_width
    product = 2 * token_count * width * slab_width

    own = call(
        norm_kernel,
        shaped((own_count, width + LANES), bf16),
        [HBM] * 4,
        [
            pltpu.SMEM((own_count,), jnp.int32),
            pltpu.SMEM((own_count,), jnp.int32),
            pltpu.VMEM((own_count, width), bf16),
            pltpu.VMEM((1, width), f32),
            pltpu.SemaphoreType.DMA((4,)),
        ],
        limit=63,
    )(correct_label_ids, included_place_flags, backbone_feature_matrix, gain)
    rows = links.gather(own)

    scaled, stats = call(
        functools.partial(logits_kernel, codes),
        (shaped((token_count, slab_width), f32), shaped((8, token_count), f32)),
        [SMEM, VMEM, VMEM],
        [pltpu.VMEM((count, own_count, LANES), f32)],
        flops=product,
        moved=head_bytes,
    )(softness_divisor, rows, output_vocab_matrix)
    tiles = links.gather_small(stats)
    parts_shape = (8, width // 4)
    scalars, parts, kept, sent = call(
        functools.partial(slab_kernel, codes, links.small_place),
        (
            shaped((8, LANES), f32),
            shaped(parts_shape, bf16),
            shaped((half, width), f32),
            shaped((half + 8, width), bf16),
        ),
        [SMEM] + [VMEM] * 5,
        [
            pltpu.VMEM((count, own_count, LANES), f32),
            pltpu.VMEM((token_count, slab_width), f32),
            pltpu.VMEM((slab_width, token_count), bf16),
            pltpu.VMEM((1, width), f32),
        ],
        flops=product,
        moved=head_bytes,
        limit=32,
    )(softness_divisor, tiles, rows, scaled, output_vocab_matrix, gain)
    twin = swap(sent, 1)

    tagged = shaped((own_count, width + parts_shape[1]), bf16)
    if count == 16:
        order = ((0, 2, 4, 3), (5, 7, 1), 6)
        kept, others, first = call(
            functools.partial(pair_kernel, order),
            (
                shaped((4 * own_count, width), f32),
                shaped((3 * own_count, width), bf16),
                tagged,
            ),
            [VMEM] * 3,
            limit=16,
        )(kept, twin, parts)
        got12 = swap(first, 2)
        got = swap(others, 2)
        second = call(functools.partial(hop_kernel, 3), tagged, [VMEM] * 3, limit=8)(
            first, got12, kept
        )
        got8 = swap(second, 4)
        third = call(functools.partial(hop_kernel, 1), tagged, [VMEM] * 4, limit=8)(
            second, got8, kept, got
        )
        last = swap(third, 8)
        b = own_count
        near = swap((kept[2 * b : 3 * b] + got[b : 2 * b].astype(f32)).astype(bf16), 4)
        more, places = [got, near], [2, 0]
    else:
        b = own_count
        kept = kept + twin[:half].astype(f32)
        gain_parts = one_value(parts.astype(f32)) + one_value(
            twin[half:, : parts_shape[1]].astype(f32)
        )
        for m in bits_of(count)[1:]:
            cut = kept.shape[0] // 2
            last = swap(kept[cut:].astype(bf16), m)
            third = two_parts(gain_parts).astype(bf16)
            arrived = swap(third, m)
            if cut > b:
                kept = kept[:cut] + last.astype(f32)
                gain_parts = one_value(third.astype(f32)) + one_value(arrived.astype(f32))
        third = jnp.concatenate([jnp.zeros((b, width), bf16), third], 1)
        last = jnp.concatenate([last, arrived], 1)
        more, places = [], []
    grad_hidden, grad_gain = call(
        functools.partial(hidden_kernel, places),
        (shaped((own_count, width), bf16), shaped((1, width), f32)),
        [VMEM] * (5 + len(more)),
        limit=8,
    )(backbone_feature_matrix, gain, kept, third, last, *more)
    return (grad_hidden, grad_gain[0], scalars[0, 1:2], scalars[0, 0:1])


def solution(mesh):
    in_specs = (
        P(("groups", "vocab"), None),
        P("groups"),
        P("groups", "vocab"),
        P("groups"),
        P(("groups", "vocab")),
        P(("groups", "vocab")),
    )
    out_specs = (P(("groups", "vocab"), None), P("groups"), P("groups"), P("groups"))
    return jax.shard_map(
        on_device, mesh=mesh, in_specs=in_specs, out_specs=out_specs, check_vma=False
    )
```

```python
import functools

import jax
import jax.numpy as jnp
from jax import lax
from jax.experimental import pallas as pl
from jax.experimental.pallas import tpu as pltpu
from jax.sharding import PartitionSpec as P

epsilon = 1e-06
f32 = jnp.float32
bf16 = jnp.bfloat16
LANES = 128
DIGIT_BITS = 7
DIGIT = 1 << DIGIT_BITS
MIB = 1 << 20
STACK_FLOPS = 20 * 10**9
REST_FLOPS = 3 * 10**9
TURN_FLOPS = 3 * 10**9


def cat(*parts):
    return jnp.concatenate(parts, 0)


def bits_of(count):
    return [1 << b for b in range(count.bit_length() - 1)]


class Links:
    def __init__(self, count):
        self.count = count

    def swap(self, value, m):
        return lax.ppermute(value, "vocab", [(i, i ^ m) for i in range(self.count)])

    def gather(self, own):
        swap = self.swap
        if self.count == 16:
            far, diagonal, near, side = swap(own, 8), swap(own, 12), swap(own, 4), swap(own, 2)
            column = stack_blocks(far, diagonal, near)
            across = swap(column, 2)
            twin = swap(cat(own, side, column), 1)
            twin_across = swap(across, 1)
            return cat(own, side, column, across, twin, twin_across), column
        blocks = own
        for m in reversed(bits_of(self.count)):
            blocks = cat(blocks, swap(blocks, m))
        return blocks, own

    def codes(self):
        if self.count == 16:
            first = [0, 2, 8, 12, 4, 10, 14, 6]
            return first + [c ^ 1 for c in first]
        codes = [0]
        for m in reversed(bits_of(self.count)):
            codes = codes + [c ^ m for c in codes]
        return codes

    def gather_small(self, own):
        swap = self.swap
        if self.count == 16:
            column = cat(own, swap(own, 12), swap(own, 8), swap(own, 4))
            return cat(column, swap(column, 3), swap(column, 2), swap(column, 1))
        tiles = own
        for m in bits_of(self.count):
            tiles = cat(tiles, swap(tiles, m))
        return tiles

    def small_place(self, code):
        if self.count == 16:
            return ((4 - (code & 3)) & 3) * 4 + ((4 - (code >> 2)) & 3)
        return code


def spec(space=pltpu.VMEM):
    return pl.BlockSpec(memory_space=space)


SMEM, VMEM, HBM = spec(pltpu.SMEM), spec(), spec(pltpu.HBM)


def call(kernel, outs, ins, scratch=(), flops=0, moved=0, limit=24):
    return pl.pallas_call(
        kernel,
        out_shape=outs,
        in_specs=ins,
        out_specs=jax.tree.map(lambda _: spec(), outs),
        scratch_shapes=list(scratch),
        compiler_params=pltpu.CompilerParams(vmem_limit_bytes=limit * MIB),
        cost_estimate=pl.CostEstimate(flops=flops, bytes_accessed=moved, transcendentals=0),
    )


def shaped(shape, dtype):
    return jax.ShapeDtypeStruct(shape, dtype)


def norm_kernel(ids_hbm, flags_hbm, rows_hbm, gain_hbm, out_ref, ids, flags, rows, gain, sems):
    copies = [
        pltpu.make_async_copy(src, dst, sems.at[k])
        for k, (src, dst) in enumerate(
            [(rows_hbm, rows), (gain_hbm, gain), (ids_hbm, ids), (flags_hbm, flags)]
        )
    ]
    for copy in copies:
        copy.start()
    for copy in copies:
        copy.wait()
    raw = rows[...].astype(f32)
    own_count, width = raw.shape
    inv_rms = lax.rsqrt(jnp.mean(raw * raw, axis=1, keepdims=True) + epsilon)
    out_ref[:, :width] = (raw * inv_rms * gain[...]).astype(bf16)
    row = lax.broadcasted_iota(jnp.int32, (own_count, LANES), 0)
    lane = lax.broadcasted_iota(jnp.int32, (own_count, LANES), 1)
    notes = jnp.zeros((own_count, LANES), jnp.int32)
    for r in range(own_count):
        label = ids[r]
        digits = (
            label & (DIGIT - 1),
            (label >> DIGIT_BITS) & (DIGIT - 1),
            label >> (2 * DIGIT_BITS),
            flags[r],
        )
        for k, digit in enumerate(digits):
            notes = jnp.where((row == r) & (lane == k), digit, notes)
    out_ref[:, width:] = notes.astype(f32).astype(bf16)


def stack_kernel(*refs):
    ins, out_ref = refs[:-1], refs[-1]
    out_ref[...] = cat(*[ref[...].astype(f32) for ref in ins]).astype(out_ref.dtype)


def stack_blocks(*blocks):
    rows, width = blocks[0].shape
    return call(
        stack_kernel,
        shaped((len(blocks) * rows, width), bf16),
        [VMEM] * len(blocks),
        flops=STACK_FLOPS,
    )(*blocks)


def fold(row):
    c = row.shape[1] // 8
    return cat(*[row[:, k * c : (k + 1) * c] for k in range(8)])


def two_parts(value):
    high = value.astype(bf16).astype(f32)
    return jnp.concatenate([high, value - high], 1)


def one_value(parts):
    c = parts.shape[1] // 2
    return parts[:, :c] + parts[:, c:]


def turn_kernel(head_ref, order_ref, out_ref):
    step = 512
    width = head_ref.shape[0]

    @pl.loop(0, width // step)
    def _(n):
        here = pl.ds(pl.multiple_of(n * step, step), step)
        out_ref[:, here] = head_ref[here, :].T


def read_notes(noted):
    label = noted[:, 0:1] + DIGIT * noted[:, 1:2] + DIGIT * DIGIT * noted[:, 2:3]
    return label.astype(jnp.int32), noted[:, 3:4]


def owned_mask(labels, me, slab_width):
    column = lax.broadcasted_iota(jnp.int32, (labels.shape[0], slab_width), 1)
    return column == labels - me * slab_width


def logits_kernel(
    codes, divisor_ref, rows_ref, head_ref, order_ref, scaled_ref, stats_ref, blocks
):
    me = lax.axis_index("vocab")
    width, slab_width = head_ref.shape
    token_count = rows_ref.shape[0]
    own_count = token_count // len(codes)
    scaled_ref[...] = (
        jnp.dot(rows_ref[:, :width], head_ref[...], preferred_element_type=f32) / divisor_ref[0]
    )
    chunk = 128
    for c in range(token_count // chunk):
        band = slice(c * chunk, (c + 1) * chunk)
        scaled = scaled_ref[band, :]
        labels, mask_f = read_notes(rows_ref[band, width:].astype(f32))
        owned = owned_mask(labels, me, slab_width)
        peak = jnp.max(scaled, axis=1, keepdims=True)
        exp_terms = jnp.exp(scaled - peak)
        columns = (
            peak,
            jnp.sum(exp_terms, axis=1, keepdims=True),
            jnp.sum(exp_terms * scaled, axis=1, keepdims=True),
            jnp.sum(jnp.where(owned, scaled, 0.0), axis=1, keepdims=True),
            mask_f,
        )
        lane = lax.broadcasted_iota(jnp.int32, (chunk, LANES), 1)
        tile = jnp.zeros((chunk, LANES), f32)
        for k, column in enumerate(columns):
            tile = jnp.where(lane == k, column, tile)
        for b in range(chunk // own_count):
            owner = me ^ codes[c * (chunk // own_count) + b]
            blocks[owner] = tile[b * own_count : (b + 1) * own_count]
    for c in range(token_count // chunk):
        per = chunk // own_count
        shared = blocks[c * per : (c + 1) * per].reshape(chunk, LANES)
        stats_ref[:, c * chunk : (c + 1) * chunk] = shared.T[:8]


def slab_kernel(
    codes,
    place,
    divisor_ref,
    tiles_ref,
    rows_ref,
    scaled_ref,
    head_ref,
    gain_ref,
    scalars_ref,
    parts_ref,
    kept_ref,
    sent_ref,
    turned,
    coefs,
):
    me = lax.axis_index("vocab")
    count = len(codes)
    slab_width, width = head_ref.shape
    token_count = rows_ref.shape[0]
    own_count = token_count // count
    half = token_count // 2

    def tile(device):
        start = place(device ^ me) * 8
        return tiles_ref[pl.ds(pl.multiple_of(start, 8), 8), :]

    peak = tile(0)[0:1]
    for j in range(1, count):
        peak = jnp.maximum(peak, tile(j)[0:1])
    totals = moments = target_z = jnp.zeros_like(peak)
    for j in range(count):
        t = tile(j)
        fade = jnp.exp(t[0:1] - peak)
        totals += t[1:2] * fade
        moments += t[2:3] * fade
        target_z += t[3:4]
    mask_f = tile(me)[4:5]
    divisor = divisor_ref[0]
    counted = jnp.maximum(jnp.sum(mask_f, axis=1, keepdims=True), 1.0)
    loss = jnp.sum(mask_f * (peak + jnp.log(totals) - target_z), axis=1, keepdims=True) / counted
    temp = -jnp.sum(mask_f * (moments / totals - target_z), axis=1, keepdims=True) / (
        counted * divisor
    )
    lane = lax.broadcasted_iota(jnp.int32, (8, LANES), 1)
    scalars_ref[...] = jnp.where(lane == 0, loss, jnp.where(lane == 1, temp, 0.0))

    factor = mask_f * (token_count / counted) / divisor
    terms = cat(peak, totals, factor, jnp.zeros((LANES - 3, token_count), f32))
    turned[...] = terms.T.reshape(count, own_count, LANES)
    chunk = 64
    per = chunk // own_count
    for c in range(token_count // chunk):
        band = slice(c * chunk, (c + 1) * chunk)
        w = cat(*[turned[me ^ code] for code in codes[c * per : (c + 1) * per]])
        labels, _ = read_notes(rows_ref[band, width:].astype(f32))
        owned = owned_mask(labels, me, slab_width).astype(f32)
        shares = jnp.exp(scaled_ref[band, :] - w[:, 0:1]) / w[:, 1:2]
        coefs[band, :] = (w[:, 2:3] * (shares - owned)).astype(bf16)
    out = jnp.dot(coefs[...], head_ref[...], preferred_element_type=f32)
    kept_ref[...] = out[:half]
    sent_ref[:half, :] = out[half:].astype(bf16)
    gain_grad = (
        jnp.sum(out * rows_ref[:, :width].astype(f32), axis=0, keepdims=True) / gain_ref[...]
    )

    parts = two_parts(fold(gain_grad)).astype(bf16)
    parts_ref[...] = parts
    sent_ref[half:, : parts.shape[1]] = parts
    sent_ref[half:, parts.shape[1] :] = jnp.zeros((8, width - parts.shape[1]), bf16)


def pair_kernel(order, own_count, kept_ref, twin_ref, *outs):
    for o, out in zip(order, outs):
        blocks = []
        for k in o:
            even = k // 2 * 2 * own_count
            band = slice(even, even + 2 * own_count)
            total = kept_ref[band, :] + twin_ref[band, :].astype(f32)
            blocks.append(total[k % 2 * own_count : (k % 2 + 1) * own_count])
        out[...] = cat(*blocks).astype(out.dtype)


def rest_kernel(order, own_count, order_ref, kept_ref, twin_ref, parts_ref, gain_out, *outs):
    pair_kernel(order, own_count, kept_ref, twin_ref, *outs)
    parts = parts_ref[...].astype(f32)
    twin_parts = twin_ref[twin_ref.shape[0] - 8 :, : parts.shape[1]].astype(f32)
    gain_sum = one_value(parts) + one_value(twin_parts)
    c = gain_out.shape[1] // 8
    for k in range(8):
        gain_out[:, k * c : (k + 1) * c] = gain_sum[k : k + 1, :]


def sum_kernel(order_ref, own_ref, near_ref, mid_ref, far_ref, out_ref):
    out_ref[...] = (own_ref[...] + near_ref[...]) + (mid_ref[...] + far_ref[...])


def hidden_kernel(rows_ref, gain_ref, kept_ref, *refs):
    more, out_ref = refs[:-1], refs[-1]
    rows = rows_ref[...].astype(f32)
    own_count, width = rows.shape
    inv_rms = lax.rsqrt(jnp.mean(rows * rows, axis=1, keepdims=True) + epsilon)
    units = rows * inv_rms
    grad = kept_ref[:own_count, :]
    for ref in more:
        grad = grad + ref[...].astype(f32)
    grad = grad * gain_ref[...]
    inner_dot = jnp.sum(grad * units, axis=1, keepdims=True)
    out_ref[...] = (inv_rms * (grad - units * inner_dot / width)).astype(bf16)


def on_device(
    backbone_feature_matrix,
    closing_rmsnorm_multiplier,
    output_vocab_matrix,
    softness_divisor,
    correct_label_ids,
    included_place_flags,
):
    count = lax.axis_size("vocab")
    links = Links(count)
    swap = links.swap
    codes = links.codes()
    own_count, width = backbone_feature_matrix.shape
    token_count = own_count * count
    half = token_count // 2
    slab_width = output_vocab_matrix.shape[1]
    gain = closing_rmsnorm_multiplier[None, :]
    head_bytes = 2 * width * slab_width
    product = 2 * token_count * width * slab_width

    own = call(
        norm_kernel,
        shaped((own_count, width + LANES), bf16),
        [HBM] * 4,
        [
            pltpu.SMEM((own_count,), jnp.int32),
            pltpu.SMEM((own_count,), jnp.int32),
            pltpu.VMEM((own_count, width), bf16),
            pltpu.VMEM((1, width), f32),
            pltpu.SemaphoreType.DMA((4,)),
        ],
        limit=63,
    )(correct_label_ids, included_place_flags, backbone_feature_matrix, gain)
    rows, early = links.gather(own)
    head_t = call(
        turn_kernel,
        shaped((slab_width, width), bf16),
        [VMEM, spec(pl.ANY)],
        flops=TURN_FLOPS,
        moved=2 * head_bytes,
        limit=4,
    )(output_vocab_matrix, early)

    scaled, stats = call(
        functools.partial(logits_kernel, codes),
        (shaped((token_count, slab_width), f32), shaped((8, token_count), f32)),
        [SMEM, VMEM, VMEM, spec(pl.ANY)],
        [pltpu.VMEM((count, own_count, LANES), f32)],
        flops=product,
        moved=head_bytes,
    )(softness_divisor, rows, output_vocab_matrix, head_t)
    tiles = links.gather_small(stats)
    parts_shape = (8, width // 4)
    scalars, parts, kept, sent = call(
        functools.partial(slab_kernel, codes, links.small_place),
        (
            shaped((8, LANES), f32),
            shaped(parts_shape, bf16),
            shaped((half, width), f32),
            shaped((half + 8, width), bf16),
        ),
        [SMEM] + [VMEM] * 5,
        [
            pltpu.VMEM((count, own_count, LANES), f32),
            pltpu.VMEM((token_count, slab_width), bf16),
        ],
        flops=product,
        moved=head_bytes,
        limit=32,
    )(softness_divisor, tiles, rows, scaled, head_t, gain)
    twin = swap(sent, 1)

    b = own_count
    if count == 16:
        going_order = (7, 5, 6)
        rest_order = ((0, 4, 2, 3), (1,))
        sizes = [(4, f32), (1, bf16)]
    else:
        quarter = count // 4
        going_order = tuple(range(quarter, 2 * quarter))
        rest_order = (tuple(range(quarter)),)
        sizes = [(quarter, f32)]
    going = call(
        functools.partial(pair_kernel, (going_order,), b),
        shaped((len(going_order) * b, width), bf16),
        [VMEM] * 2,
    )(kept, twin)
    gain_grad, kept, *rest = call(
        functools.partial(rest_kernel, rest_order, b),
        (shaped((1, width), f32),) + tuple(shaped((k * b, width), t) for k, t in sizes),
        [spec(pl.ANY)] + [VMEM] * 3,
        flops=REST_FLOPS,
    )(going, kept, twin, parts)
    if count == 16:
        crossed = swap(going, 2)
        beside = swap(rest[0], 2)
        gain_far, gain_mid, gain_near = [swap(gain_grad, m) for m in (12, 8, 4)]
        gain_grad = call(
            sum_kernel, shaped((1, width), f32), [spec(pl.ANY)] + [VMEM] * 4, limit=8
        )(crossed, gain_grad, gain_near, gain_mid, gain_far)
        gain_grad = gain_grad + swap(gain_grad, 2)
        column = (kept[b:] + crossed.astype(f32)).astype(bf16)
        more = [beside] + [
            swap(column[k * b : (k + 1) * b], m) for k, m in ((2, 12), (1, 8), (0, 4))
        ]
    else:
        for m in bits_of(count)[1:]:
            gain_grad = gain_grad + swap(gain_grad, m)
        for m in bits_of(count)[1:-1]:
            kept = kept + swap(going, m).astype(f32)
            cut = kept.shape[0] // 2
            kept, going = kept[:cut], kept[cut:].astype(bf16)
        more = [swap(going, count // 2)]
    grad_hidden = call(
        hidden_kernel, shaped((b, width), bf16), [VMEM] * (3 + len(more)), limit=8
    )(backbone_feature_matrix, gain, kept, *more)
    return (grad_hidden, gain_grad[0], scalars[0, 1:2], scalars[0, 0:1])


def solution(mesh):
    in_specs = (
        P(("groups", "vocab"), None),
        P("groups"),
        P("groups", "vocab"),
        P("groups"),
        P(("groups", "vocab")),
        P(("groups", "vocab")),
    )
    out_specs = (P(("groups", "vocab"), None), P("groups"), P("groups"), P("groups"))
    return jax.shard_map(
        on_device, mesh=mesh, in_specs=in_specs, out_specs=out_specs, check_vma=False
    )
```

```python
import functools

import jax
import jax.numpy as jnp
from jax import lax
from jax.experimental import pallas as pl
from jax.experimental.pallas import tpu as pltpu
from jax.sharding import PartitionSpec as P

epsilon = 1e-06
f32 = jnp.float32
bf16 = jnp.bfloat16
LANES = 128
DIGIT_BITS = 7
DIGIT = 1 << DIGIT_BITS
MIB = 1 << 20
STACK_FLOPS = 20 * 10**9
REST_FLOPS = 3 * 10**9
TURN_FLOPS = 3 * 10**9


def cat(*parts):
    return jnp.concatenate(parts, 0)


def bits_of(count):
    return [1 << b for b in range(count.bit_length() - 1)]


class Links:
    def __init__(self, count):
        self.count = count

    def swap(self, value, m):
        return lax.ppermute(value, "vocab", [(i, i ^ m) for i in range(self.count)])

    def gather(self, own, meanwhile):
        swap = self.swap
        if self.count == 16:
            far, near, side = swap(own, 8), swap(own, 4), swap(own, 2)
            across = stack_blocks([far, near], flops=STACK_FLOPS)
            crossed = swap(across, 2)
            beyond, diagonal = swap(side, 12), swap(far, 4)
            result = meanwhile(across)
            chips = stack_blocks([own, side, far, near, beyond, diagonal, crossed], after=result)
            return cat(chips, swap(chips, 1)), result
        blocks, result = own, meanwhile(own)
        for m in reversed(bits_of(self.count)):
            blocks = cat(blocks, swap(blocks, m))
        return blocks, result

    def codes(self):
        if self.count == 16:
            first = [0, 2, 8, 4, 14, 12, 10, 6]
            return first + [c ^ 1 for c in first]
        codes = [0]
        for m in reversed(bits_of(self.count)):
            codes = codes + [c ^ m for c in codes]
        return codes

    def gather_small(self, own, meanwhile):
        swap = self.swap
        result = meanwhile(own)
        if self.count == 16:
            far = [swap(own, m) for m in (12, 8, 4)]
            column = stack_blocks([own] + far, after=result)
            return cat(column, swap(column, 3), swap(column, 2), swap(column, 1)), result
        tiles = own
        for m in bits_of(self.count):
            tiles = cat(tiles, swap(tiles, m))
        return tiles, result

    def small_place(self, code):
        if self.count == 16:
            return ((4 - (code & 3)) & 3) * 4 + ((4 - (code >> 2)) & 3)
        return code


def spec(space=pltpu.VMEM):
    return pl.BlockSpec(memory_space=space)


SMEM, VMEM, HBM = spec(pltpu.SMEM), spec(), spec(pltpu.HBM)


def call(kernel, outs, ins, scratch=(), flops=0, moved=0, limit=20):
    return pl.pallas_call(
        kernel,
        out_shape=outs,
        in_specs=ins,
        out_specs=jax.tree.map(lambda _: spec(), outs),
        scratch_shapes=list(scratch),
        compiler_params=pltpu.CompilerParams(vmem_limit_bytes=limit * MIB),
        cost_estimate=pl.CostEstimate(flops=flops, bytes_accessed=moved, transcendentals=0),
    )


def shaped(shape, dtype):
    return jax.ShapeDtypeStruct(shape, dtype)


def norm_kernel(ids_hbm, flags_hbm, rows_hbm, gain_hbm, out_ref, ids, flags, rows, gain, sems):
    copies = [
        pltpu.make_async_copy(src, dst, sems.at[k])
        for k, (src, dst) in enumerate(
            [(rows_hbm, rows), (gain_hbm, gain), (ids_hbm, ids), (flags_hbm, flags)]
        )
    ]
    for copy in copies:
        copy.start()
    for copy in copies:
        copy.wait()
    raw = rows[...].astype(f32)
    own_count, width = raw.shape
    inv_rms = lax.rsqrt(jnp.mean(raw * raw, axis=1, keepdims=True) + epsilon)
    out_ref[:, :width] = (raw * inv_rms * gain[...]).astype(bf16)
    row = lax.broadcasted_iota(jnp.int32, (own_count, LANES), 0)
    lane = lax.broadcasted_iota(jnp.int32, (own_count, LANES), 1)
    notes = jnp.zeros((own_count, LANES), jnp.int32)
    for r in range(own_count):
        label = ids[r]
        digits = (
            label & (DIGIT - 1),
            (label >> DIGIT_BITS) & (DIGIT - 1),
            label >> (2 * DIGIT_BITS),
            flags[r],
        )
        for k, digit in enumerate(digits):
            notes = jnp.where((row == r) & (lane == k), digit, notes)
    out_ref[:, width:] = notes.astype(f32).astype(bf16)


def stack_kernel(count, *refs):
    refs[-1][...] = cat(*[ref[...].astype(f32) for ref in refs[:count]]).astype(refs[-1].dtype)


def stack_blocks(blocks, after=None, flops=0):
    rows = sum(block.shape[0] for block in blocks)
    more = [] if after is None else [after]
    return call(
        functools.partial(stack_kernel, len(blocks)),
        shaped((rows, blocks[0].shape[1]), blocks[0].dtype),
        [VMEM] * len(blocks) + [spec(pl.ANY)] * len(more),
        flops=flops,
        limit=8,
    )(*blocks, *more)


def fold(row):
    c = row.shape[1] // 8
    return cat(*[row[:, k * c : (k + 1) * c] for k in range(8)])


def two_parts(value):
    high = value.astype(bf16).astype(f32)
    return jnp.concatenate([high, value - high], 1)


def one_value(parts):
    c = parts.shape[1] // 2
    return parts[:, :c] + parts[:, c:]


def turn_kernel(part, head_ref, order_ref, out_ref):
    step = 512
    width = head_ref.shape[0]
    rows = out_ref.shape[0]

    @pl.loop(0, width // step)
    def _(n):
        here = pl.ds(pl.multiple_of(n * step, step), step)
        out_ref[:, here] = head_ref[here, part * rows : (part + 1) * rows].T


def read_notes(noted):
    label = noted[:, 0:1] + DIGIT * noted[:, 1:2] + DIGIT * DIGIT * noted[:, 2:3]
    return label.astype(jnp.int32), noted[:, 3:4]


def owned_mask(labels, me, slab_width):
    column = lax.broadcasted_iota(jnp.int32, (labels.shape[0], slab_width), 1)
    return column == labels - me * slab_width


def logits_kernel(
    codes, divisor_ref, rows_ref, head_ref, order_ref, scaled_ref, stats_ref, blocks
):
    me = lax.axis_index("vocab")
    width, slab_width = head_ref.shape
    token_count = rows_ref.shape[0]
    own_count = token_count // len(codes)
    scaled_ref[...] = (
        jnp.dot(rows_ref[:, :width], head_ref[...], preferred_element_type=f32) / divisor_ref[0]
    )
    chunk = 128
    for c in range(token_count // chunk):
        band = slice(c * chunk, (c + 1) * chunk)
        scaled = scaled_ref[band, :]
        labels, mask_f = read_notes(rows_ref[band, width:].astype(f32))
        owned = owned_mask(labels, me, slab_width)
        peak = jnp.max(scaled, axis=1, keepdims=True)
        exp_terms = jnp.exp(scaled - peak)
        columns = (
            peak,
            jnp.sum(exp_terms, axis=1, keepdims=True),
            jnp.sum(exp_terms * scaled, axis=1, keepdims=True),
            jnp.sum(jnp.where(owned, scaled, 0.0), axis=1, keepdims=True),
            mask_f,
        )
        lane = lax.broadcasted_iota(jnp.int32, (chunk, LANES), 1)
        tile = jnp.zeros((chunk, LANES), f32)
        for k, column in enumerate(columns):
            tile = jnp.where(lane == k, column, tile)
        for b in range(chunk // own_count):
            owner = me ^ codes[c * (chunk // own_count) + b]
            blocks[owner] = tile[b * own_count : (b + 1) * own_count]
    for c in range(token_count // chunk):
        per = chunk // own_count
        shared = blocks[c * per : (c + 1) * per].reshape(chunk, LANES)
        stats_ref[:, c * chunk : (c + 1) * chunk] = shared.T[:8]


def slab_kernel(
    codes,
    place,
    divisor_ref,
    tiles_ref,
    rows_ref,
    scaled_ref,
    head_ref,
    head2_ref,
    gain_ref,
    scalars_ref,
    parts_ref,
    kept_ref,
    sent_ref,
    turned,
    coefs,
):
    me = lax.axis_index("vocab")
    count = len(codes)
    width = head_ref.shape[1]
    cut, slab_width = head_ref.shape[0], 2 * head_ref.shape[0]
    token_count = rows_ref.shape[0]
    own_count = token_count // count
    half = token_count // 2

    def tile(device):
        start = place(device ^ me) * 8
        return tiles_ref[pl.ds(pl.multiple_of(start, 8), 8), :]

    peak = tile(0)[0:1]
    for j in range(1, count):
        peak = jnp.maximum(peak, tile(j)[0:1])
    totals = moments = target_z = jnp.zeros_like(peak)
    for j in range(count):
        t = tile(j)
        fade = jnp.exp(t[0:1] - peak)
        totals += t[1:2] * fade
        moments += t[2:3] * fade
        target_z += t[3:4]
    mask_f = tile(me)[4:5]
    divisor = divisor_ref[0]
    counted = jnp.maximum(jnp.sum(mask_f, axis=1, keepdims=True), 1.0)
    loss = jnp.sum(mask_f * (peak + jnp.log(totals) - target_z), axis=1, keepdims=True) / counted
    temp = -jnp.sum(mask_f * (moments / totals - target_z), axis=1, keepdims=True) / (
        counted * divisor
    )
    lane = lax.broadcasted_iota(jnp.int32, (8, LANES), 1)
    scalars_ref[...] = jnp.where(lane == 0, loss, jnp.where(lane == 1, temp, 0.0))

    factor = mask_f * (token_count / counted) / divisor
    terms = cat(peak, totals, factor, jnp.zeros((LANES - 3, token_count), f32))
    turned[...] = terms.T.reshape(count, own_count, LANES)
    chunk = 64
    per = chunk // own_count
    for c in range(token_count // chunk):
        band = slice(c * chunk, (c + 1) * chunk)
        w = cat(*[turned[me ^ code] for code in codes[c * per : (c + 1) * per]])
        labels, _ = read_notes(rows_ref[band, width:].astype(f32))
        owned = owned_mask(labels, me, slab_width).astype(f32)
        shares = jnp.exp(scaled_ref[band, :] - w[:, 0:1]) / w[:, 1:2]
        coefs[band, :] = (w[:, 2:3] * (shares - owned)).astype(bf16)
    out = jnp.dot(coefs[:, :cut], head_ref[...], preferred_element_type=f32) + jnp.dot(
        coefs[:, cut:], head2_ref[...], preferred_element_type=f32
    )
    kept_ref[...] = out[:half]
    sent_ref[:half, :] = out[half:].astype(bf16)
    gain_grad = (
        jnp.sum(out * rows_ref[:, :width].astype(f32), axis=0, keepdims=True) / gain_ref[...]
    )

    parts = two_parts(fold(gain_grad)).astype(bf16)
    parts_ref[...] = parts
    sent_ref[half:, : parts.shape[1]] = parts
    sent_ref[half:, parts.shape[1] :] = jnp.zeros((8, width - parts.shape[1]), bf16)


def pair_kernel(order, own_count, kept_ref, twin_ref, *outs):
    for o, out in zip(order, outs):
        blocks = []
        for k in o:
            even = k // 2 * 2 * own_count
            band = slice(even, even + 2 * own_count)
            total = kept_ref[band, :] + twin_ref[band, :].astype(f32)
            blocks.append(total[k % 2 * own_count : (k % 2 + 1) * own_count])
        out[...] = cat(*blocks).astype(out.dtype)


def rest_kernel(order, own_count, order_ref, kept_ref, twin_ref, parts_ref, gain_out, *outs):
    pair_kernel(order, own_count, kept_ref, twin_ref, *outs)
    parts = parts_ref[...].astype(f32)
    twin_parts = twin_ref[twin_ref.shape[0] - 8 :, : parts.shape[1]].astype(f32)
    gain_sum = one_value(parts) + one_value(twin_parts)
    c = gain_out.shape[1] // 8
    for k in range(8):
        gain_out[:, k * c : (k + 1) * c] = gain_sum[k : k + 1, :]


def sum_kernel(order_ref, own_ref, near_ref, mid_ref, far_ref, out_ref):
    out_ref[...] = (own_ref[...] + near_ref[...]) + (mid_ref[...] + far_ref[...])


def hidden_kernel(rows_ref, gain_ref, kept_ref, *refs):
    more, out_ref = refs[:-1], refs[-1]
    rows = rows_ref[...].astype(f32)
    own_count, width = rows.shape
    inv_rms = lax.rsqrt(jnp.mean(rows * rows, axis=1, keepdims=True) + epsilon)
    units = rows * inv_rms
    grad = kept_ref[:own_count, :]
    for ref in more:
        grad = grad + ref[...].astype(f32)
    grad = grad * gain_ref[...]
    inner_dot = jnp.sum(grad * units, axis=1, keepdims=True)
    out_ref[...] = (inv_rms * (grad - units * inner_dot / width)).astype(bf16)


def on_device(
    backbone_feature_matrix,
    closing_rmsnorm_multiplier,
    output_vocab_matrix,
    softness_divisor,
    correct_label_ids,
    included_place_flags,
):
    count = lax.axis_size("vocab")
    links = Links(count)
    swap = links.swap
    codes = links.codes()
    own_count, width = backbone_feature_matrix.shape
    token_count = own_count * count
    half = token_count // 2
    slab_width = output_vocab_matrix.shape[1]
    gain = closing_rmsnorm_multiplier[None, :]
    head_bytes = 2 * width * slab_width
    product = 2 * token_count * width * slab_width

    own = call(
        norm_kernel,
        shaped((own_count, width + LANES), bf16),
        [HBM] * 4,
        [
            pltpu.SMEM((own_count,), jnp.int32),
            pltpu.SMEM((own_count,), jnp.int32),
            pltpu.VMEM((own_count, width), bf16),
            pltpu.VMEM((1, width), f32),
            pltpu.SemaphoreType.DMA((4,)),
        ],
        limit=63,
    )(correct_label_ids, included_place_flags, backbone_feature_matrix, gain)
    def turn(order, part):
        return call(
            functools.partial(turn_kernel, part),
            shaped((slab_width // 2, width), bf16),
            [VMEM, spec(pl.ANY)],
            flops=TURN_FLOPS,
            moved=head_bytes,
            limit=4,
        )(output_vocab_matrix, order)

    rows, left = links.gather(own, lambda order: turn(order, 0))

    scaled, stats = call(
        functools.partial(logits_kernel, codes),
        (shaped((token_count, slab_width), f32), shaped((8, token_count), f32)),
        [SMEM, VMEM, VMEM, spec(pl.ANY)],
        [pltpu.VMEM((count, own_count, LANES), f32)],
        flops=product,
        moved=head_bytes,
    )(softness_divisor, rows, output_vocab_matrix, left)
    tiles, right = links.gather_small(stats, lambda order: turn(order, 1))
    parts_shape = (8, width // 4)
    scalars, parts, kept, sent = call(
        functools.partial(slab_kernel, codes, links.small_place),
        (
            shaped((8, LANES), f32),
            shaped(parts_shape, bf16),
            shaped((half, width), f32),
            shaped((half + 8, width), bf16),
        ),
        [SMEM] + [VMEM] * 6,
        [
            pltpu.VMEM((count, own_count, LANES), f32),
            pltpu.VMEM((token_count, slab_width), bf16),
        ],
        flops=product,
        moved=head_bytes,
        limit=28,
    )(softness_divisor, tiles, rows, scaled, left, right, gain)
    twin = swap(sent, 1)

    b = own_count
    if count == 16:
        going_order = (7, 6, 4)
        rest_order = ((0, 3, 2, 5), (1,))
        sizes = [(4, f32), (1, bf16)]
    else:
        quarter = count // 4
        going_order = tuple(range(quarter, 2 * quarter))
        rest_order = (tuple(range(quarter)),)
        sizes = [(quarter, f32)]
    going = call(
        functools.partial(pair_kernel, (going_order,), b),
        shaped((len(going_order) * b, width), bf16),
        [VMEM] * 2,
    )(kept, twin)
    gain_grad, kept, *rest = call(
        functools.partial(rest_kernel, rest_order, b),
        (shaped((1, width), f32),) + tuple(shaped((k * b, width), t) for k, t in sizes),
        [spec(pl.ANY)] + [VMEM] * 3,
        flops=REST_FLOPS,
    )(going, kept, twin, parts)
    if count == 16:
        crossed = swap(going, 2)
        beside = swap(rest[0], 2)
        gain_far, gain_mid, gain_near = [swap(gain_grad, m) for m in (12, 8, 4)]
        gain_grad = call(
            sum_kernel, shaped((1, width), f32), [spec(pl.ANY)] + [VMEM] * 4, limit=8
        )(crossed, gain_grad, gain_near, gain_mid, gain_far)
        gain_grad = gain_grad + swap(gain_grad, 2)
        column = (kept[b:] + crossed.astype(f32)).astype(bf16)
        more = [beside] + [
            swap(column[k * b : (k + 1) * b], m) for k, m in ((2, 12), (1, 8), (0, 4))
        ]
    else:
        for m in bits_of(count)[1:]:
            gain_grad = gain_grad + swap(gain_grad, m)
        for m in bits_of(count)[1:-1]:
            kept = kept + swap(going, m).astype(f32)
            cut = kept.shape[0] // 2
            kept, going = kept[:cut], kept[cut:].astype(bf16)
        more = [swap(going, count // 2)]
    grad_hidden = call(
        hidden_kernel, shaped((b, width), bf16), [VMEM] * (3 + len(more)), limit=8
    )(backbone_feature_matrix, gain, kept, *more)
    return (grad_hidden, gain_grad[0], scalars[0, 1:2], scalars[0, 0:1])


def solution(mesh):
    in_specs = (
        P(("groups", "vocab"), None),
        P("groups"),
        P("groups", "vocab"),
        P("groups"),
        P(("groups", "vocab")),
        P(("groups", "vocab")),
    )
    out_specs = (P(("groups", "vocab"), None), P("groups"), P("groups"), P("groups"))
    return jax.shard_map(
        on_device, mesh=mesh, in_specs=in_specs, out_specs=out_specs, check_vma=False
    )
```

```python
import functools

import jax
import jax.numpy as jnp
from jax import lax
from jax.experimental import pallas as pl
from jax.experimental.pallas import tpu as pltpu
from jax.sharding import PartitionSpec as P

epsilon = 1e-06
f32 = jnp.float32
bf16 = jnp.bfloat16
LANES = 128
DIGIT_BITS = 7
DIGIT = 1 << DIGIT_BITS
MIB = 1 << 20
STACK_FLOPS = 20 * 10**9
REST_FLOPS = 3 * 10**9
TURN_FLOPS = 3 * 10**9


def cat(*parts):
    return jnp.concatenate(parts, 0)


def bits_of(count):
    return [1 << b for b in range(count.bit_length() - 1)]


class Links:
    def __init__(self, count):
        self.count = count

    def swap(self, value, m):
        return lax.ppermute(value, "vocab", [(i, i ^ m) for i in range(self.count)])

    def gather(self, own, meanwhile):
        swap = self.swap
        if self.count == 16:
            far, near, side = swap(own, 8), swap(own, 4), swap(own, 2)
            across = stack_blocks([near, far], flops=STACK_FLOPS)
            crossed = swap(across, 2)
            beyond, diagonal = swap(side, 12), swap(far, 4)
            result = meanwhile(across)
            chips = stack_blocks([own, side, far, near, beyond, diagonal, crossed], after=result)
            return cat(chips, swap(chips, 1)), result
        blocks, result = own, meanwhile(own)
        for m in reversed(bits_of(self.count)):
            blocks = cat(blocks, swap(blocks, m))
        return blocks, result

    def codes(self):
        if self.count == 16:
            first = [0, 2, 8, 4, 14, 12, 6, 10]
            return first + [c ^ 1 for c in first]
        codes = [0]
        for m in reversed(bits_of(self.count)):
            codes = codes + [c ^ m for c in codes]
        return codes

    def gather_small(self, own, meanwhile):
        swap = self.swap
        result = meanwhile(own)
        if self.count == 16:
            others = [swap(own, m) for m in (4, 8, 12)]
            column = stack_blocks([own] + others, after=result)
            return cat(column, swap(column, 1), swap(column, 2), swap(column, 3)), result
        tiles = own
        for m in bits_of(self.count):
            tiles = cat(tiles, swap(tiles, m))
        return tiles, result

    def small_place(self, code):
        if self.count == 16:
            return (code & 3) * 4 + (code >> 2)
        return code


def spec(space=pltpu.VMEM):
    return pl.BlockSpec(memory_space=space)


SMEM, VMEM, HBM = spec(pltpu.SMEM), spec(), spec(pltpu.HBM)


def call(kernel, outs, ins, scratch=(), flops=0, moved=0, limit=20):
    return pl.pallas_call(
        kernel,
        out_shape=outs,
        in_specs=ins,
        out_specs=jax.tree.map(lambda _: spec(), outs),
        scratch_shapes=list(scratch),
        compiler_params=pltpu.CompilerParams(vmem_limit_bytes=limit * MIB),
        cost_estimate=pl.CostEstimate(flops=flops, bytes_accessed=moved, transcendentals=0),
    )


def shaped(shape, dtype):
    return jax.ShapeDtypeStruct(shape, dtype)


def norm_kernel(ids_hbm, flags_hbm, rows_hbm, gain_hbm, out_ref, ids, flags, rows, gain, sems):
    copies = [
        pltpu.make_async_copy(src, dst, sems.at[k])
        for k, (src, dst) in enumerate(
            [(rows_hbm, rows), (gain_hbm, gain), (ids_hbm, ids), (flags_hbm, flags)]
        )
    ]
    for copy in copies:
        copy.start()
    for copy in copies:
        copy.wait()
    raw = rows[...].astype(f32)
    own_count, width = raw.shape
    inv_rms = lax.rsqrt(jnp.mean(raw * raw, axis=1, keepdims=True) + epsilon)
    out_ref[:, :width] = (raw * inv_rms * gain[...]).astype(bf16)
    row = lax.broadcasted_iota(jnp.int32, (own_count, LANES), 0)
    lane = lax.broadcasted_iota(jnp.int32, (own_count, LANES), 1)
    notes = jnp.zeros((own_count, LANES), jnp.int32)
    for r in range(own_count):
        label = ids[r]
        digits = (
            label & (DIGIT - 1),
            (label >> DIGIT_BITS) & (DIGIT - 1),
            label >> (2 * DIGIT_BITS),
            flags[r],
        )
        for k, digit in enumerate(digits):
            notes = jnp.where((row == r) & (lane == k), digit, notes)
    out_ref[:, width:] = notes.astype(f32).astype(bf16)


def stack_kernel(count, *refs):
    refs[-1][...] = cat(*[ref[...].astype(f32) for ref in refs[:count]]).astype(refs[-1].dtype)


def stack_blocks(blocks, after=None, flops=0):
    rows = sum(block.shape[0] for block in blocks)
    more = [] if after is None else [after]
    return call(
        functools.partial(stack_kernel, len(blocks)),
        shaped((rows, blocks[0].shape[1]), blocks[0].dtype),
        [VMEM] * len(blocks) + [spec(pl.ANY)] * len(more),
        flops=flops,
        limit=8,
    )(*blocks, *more)


def fold(row):
    c = row.shape[1] // 8
    return cat(*[row[:, k * c : (k + 1) * c] for k in range(8)])


def two_parts(value):
    high = value.astype(bf16).astype(f32)
    return jnp.concatenate([high, value - high], 1)


def one_value(parts):
    c = parts.shape[1] // 2
    return parts[:, :c] + parts[:, c:]


def turn_kernel(part, head_ref, order_ref, out_ref):
    step = 512
    width = head_ref.shape[0]
    rows = out_ref.shape[0]

    @pl.loop(0, width // step)
    def _(n):
        here = pl.ds(pl.multiple_of(n * step, step), step)
        out_ref[:, here] = head_ref[here, part * rows : (part + 1) * rows].T


def read_notes(noted):
    label = noted[:, 0:1] + DIGIT * noted[:, 1:2] + DIGIT * DIGIT * noted[:, 2:3]
    return label.astype(jnp.int32), noted[:, 3:4]


def owned_mask(labels, me, slab_width):
    column = lax.broadcasted_iota(jnp.int32, (labels.shape[0], slab_width), 1)
    return column == labels - me * slab_width


def logits_kernel(
    codes, divisor_ref, rows_ref, head_ref, order_ref, scaled_ref, stats_ref, blocks
):
    me = lax.axis_index("vocab")
    width, slab_width = head_ref.shape
    token_count = rows_ref.shape[0]
    own_count = token_count // len(codes)
    scaled_ref[...] = (
        jnp.dot(rows_ref[:, :width], head_ref[...], preferred_element_type=f32) / divisor_ref[0]
    )
    chunk = 128
    for c in range(token_count // chunk):
        band = slice(c * chunk, (c + 1) * chunk)
        scaled = scaled_ref[band, :]
        labels, mask_f = read_notes(rows_ref[band, width:].astype(f32))
        owned = owned_mask(labels, me, slab_width)
        peak = jnp.max(scaled, axis=1, keepdims=True)
        exp_terms = jnp.exp(scaled - peak)
        columns = (
            peak,
            jnp.sum(exp_terms, axis=1, keepdims=True),
            jnp.sum(exp_terms * scaled, axis=1, keepdims=True),
            jnp.sum(jnp.where(owned, scaled, 0.0), axis=1, keepdims=True),
            mask_f,
        )
        lane = lax.broadcasted_iota(jnp.int32, (chunk, LANES), 1)
        tile = jnp.zeros((chunk, LANES), f32)
        for k, column in enumerate(columns):
            tile = jnp.where(lane == k, column, tile)
        for b in range(chunk // own_count):
            owner = me ^ codes[c * (chunk // own_count) + b]
            blocks[owner] = tile[b * own_count : (b + 1) * own_count]
    for c in range(token_count // chunk):
        per = chunk // own_count
        shared = blocks[c * per : (c + 1) * per].reshape(chunk, LANES)
        stats_ref[:, c * chunk : (c + 1) * chunk] = shared.T[:8]


def slab_kernel(
    codes,
    place,
    divisor_ref,
    tiles_ref,
    rows_ref,
    scaled_ref,
    head_ref,
    head2_ref,
    gain_ref,
    scalars_ref,
    parts_ref,
    kept_ref,
    sent_ref,
    turned,
    coefs,
):
    me = lax.axis_index("vocab")
    count = len(codes)
    width = head_ref.shape[1]
    cut, slab_width = head_ref.shape[0], 2 * head_ref.shape[0]
    token_count = rows_ref.shape[0]
    own_count = token_count // count
    half = token_count // 2

    def tile(device):
        start = place(device ^ me) * 8
        return tiles_ref[pl.ds(pl.multiple_of(start, 8), 8), :]

    peak = tile(0)[0:1]
    for j in range(1, count):
        peak = jnp.maximum(peak, tile(j)[0:1])
    totals = moments = target_z = jnp.zeros_like(peak)
    for j in range(count):
        t = tile(j)
        fade = jnp.exp(t[0:1] - peak)
        totals += t[1:2] * fade
        moments += t[2:3] * fade
        target_z += t[3:4]
    mask_f = tile(me)[4:5]
    divisor = divisor_ref[0]
    counted = jnp.maximum(jnp.sum(mask_f, axis=1, keepdims=True), 1.0)
    loss = jnp.sum(mask_f * (peak + jnp.log(totals) - target_z), axis=1, keepdims=True) / counted
    temp = -jnp.sum(mask_f * (moments / totals - target_z), axis=1, keepdims=True) / (
        counted * divisor
    )
    lane = lax.broadcasted_iota(jnp.int32, (8, LANES), 1)
    scalars_ref[...] = jnp.where(lane == 0, loss, jnp.where(lane == 1, temp, 0.0))

    factor = mask_f * (token_count / counted) / divisor
    terms = cat(peak, totals, factor, jnp.zeros((LANES - 3, token_count), f32))
    turned[...] = terms.T.reshape(count, own_count, LANES)
    chunk = 64
    per = chunk // own_count
    for c in range(token_count // chunk):
        band = slice(c * chunk, (c + 1) * chunk)
        w = cat(*[turned[me ^ code] for code in codes[c * per : (c + 1) * per]])
        labels, _ = read_notes(rows_ref[band, width:].astype(f32))
        owned = owned_mask(labels, me, slab_width).astype(f32)
        shares = jnp.exp(scaled_ref[band, :] - w[:, 0:1]) / w[:, 1:2]
        coefs[band, :] = (w[:, 2:3] * (shares - owned)).astype(bf16)
    out = jnp.dot(coefs[:, :cut], head_ref[...], preferred_element_type=f32) + jnp.dot(
        coefs[:, cut:], head2_ref[...], preferred_element_type=f32
    )
    kept_ref[...] = out[:half]
    sent_ref[:half, :] = out[half:].astype(bf16)
    gain_grad = (
        jnp.sum(out * rows_ref[:, :width].astype(f32), axis=0, keepdims=True) / gain_ref[...]
    )

    parts = two_parts(fold(gain_grad)).astype(bf16)
    parts_ref[...] = parts
    sent_ref[half:, : parts.shape[1]] = parts
    sent_ref[half:, parts.shape[1] :] = jnp.zeros((8, width - parts.shape[1]), bf16)


def pair_kernel(order, own_count, kept_ref, twin_ref, *outs):
    for o, out in zip(order, outs):
        blocks = []
        for k in o:
            even = k // 2 * 2 * own_count
            band = slice(even, even + 2 * own_count)
            total = kept_ref[band, :] + twin_ref[band, :].astype(f32)
            blocks.append(total[k % 2 * own_count : (k % 2 + 1) * own_count])
        out[...] = cat(*blocks).astype(out.dtype)


def rest_kernel(order, own_count, order_ref, kept_ref, twin_ref, parts_ref, gain_out, *outs):
    pair_kernel(order, own_count, kept_ref, twin_ref, *outs)
    parts = parts_ref[...].astype(f32)
    twin_parts = twin_ref[twin_ref.shape[0] - 8 :, : parts.shape[1]].astype(f32)
    gain_sum = one_value(parts) + one_value(twin_parts)
    c = gain_out.shape[1] // 8
    for k in range(8):
        gain_out[:, k * c : (k + 1) * c] = gain_sum[k : k + 1, :]


def sum_kernel(order_ref, own_ref, near_ref, mid_ref, far_ref, out_ref):
    out_ref[...] = (own_ref[...] + near_ref[...]) + (mid_ref[...] + far_ref[...])


def hidden_kernel(rows_ref, gain_ref, kept_ref, *refs):
    more, out_ref = refs[:-1], refs[-1]
    rows = rows_ref[...].astype(f32)
    own_count, width = rows.shape
    inv_rms = lax.rsqrt(jnp.mean(rows * rows, axis=1, keepdims=True) + epsilon)
    units = rows * inv_rms
    grad = kept_ref[:own_count, :]
    for ref in more:
        grad = grad + ref[...].astype(f32)
    grad = grad * gain_ref[...]
    inner_dot = jnp.sum(grad * units, axis=1, keepdims=True)
    out_ref[...] = (inv_rms * (grad - units * inner_dot / width)).astype(bf16)


def on_device(
    backbone_feature_matrix,
    closing_rmsnorm_multiplier,
    output_vocab_matrix,
    softness_divisor,
    correct_label_ids,
    included_place_flags,
):
    count = lax.axis_size("vocab")
    links = Links(count)
    swap = links.swap
    codes = links.codes()
    own_count, width = backbone_feature_matrix.shape
    token_count = own_count * count
    half = token_count // 2
    slab_width = output_vocab_matrix.shape[1]
    gain = closing_rmsnorm_multiplier[None, :]
    head_bytes = 2 * width * slab_width
    product = 2 * token_count * width * slab_width

    own = call(
        norm_kernel,
        shaped((own_count, width + LANES), bf16),
        [HBM] * 4,
        [
            pltpu.SMEM((own_count,), jnp.int32),
            pltpu.SMEM((own_count,), jnp.int32),
            pltpu.VMEM((own_count, width), bf16),
            pltpu.VMEM((1, width), f32),
            pltpu.SemaphoreType.DMA((4,)),
        ],
        limit=63,
    )(correct_label_ids, included_place_flags, backbone_feature_matrix, gain)
    def turn(order, part):
        return call(
            functools.partial(turn_kernel, part),
            shaped((slab_width // 2, width), bf16),
            [VMEM, spec(pl.ANY)],
            flops=TURN_FLOPS,
            moved=head_bytes,
            limit=4,
        )(output_vocab_matrix, order)

    rows, left = links.gather(own, lambda order: turn(order, 0))

    scaled, stats = call(
        functools.partial(logits_kernel, codes),
        (shaped((token_count, slab_width), f32), shaped((8, token_count), f32)),
        [SMEM, VMEM, VMEM, spec(pl.ANY)],
        [pltpu.VMEM((count, own_count, LANES), f32)],
        flops=product,
        moved=head_bytes,
    )(softness_divisor, rows, output_vocab_matrix, left)
    tiles, right = links.gather_small(stats, lambda order: turn(order, 1))
    parts_shape = (8, width // 4)
    scalars, parts, kept, sent = call(
        functools.partial(slab_kernel, codes, links.small_place),
        (
            shaped((8, LANES), f32),
            shaped(parts_shape, bf16),
            shaped((half, width), f32),
            shaped((half + 8, width), bf16),
        ),
        [SMEM] + [VMEM] * 6,
        [
            pltpu.VMEM((count, own_count, LANES), f32),
            pltpu.VMEM((token_count, slab_width), bf16),
        ],
        flops=product,
        moved=head_bytes,
        limit=28,
    )(softness_divisor, tiles, rows, scaled, left, right, gain)
    twin = swap(sent, 1)

    b = own_count
    if count == 16:
        going_order = (6, 7, 4)
        rest_order = ((0, 3, 2, 5), (1,))
        sizes = [(4, f32), (1, bf16)]
    else:
        quarter = count // 4
        going_order = tuple(range(quarter, 2 * quarter))
        rest_order = (tuple(range(quarter)),)
        sizes = [(quarter, f32)]
    going = call(
        functools.partial(pair_kernel, (going_order,), b),
        shaped((len(going_order) * b, width), bf16),
        [VMEM] * 2,
    )(kept, twin)
    gain_grad, kept, *rest = call(
        functools.partial(rest_kernel, rest_order, b),
        (shaped((1, width), f32),) + tuple(shaped((k * b, width), t) for k, t in sizes),
        [spec(pl.ANY)] + [VMEM] * 3,
        flops=REST_FLOPS,
    )(going, kept, twin, parts)
    if count == 16:
        crossed = swap(going, 2)
        beside = swap(rest[0], 2)
        gain_far, gain_mid, gain_near = [swap(gain_grad, m) for m in (12, 8, 4)]
        gain_grad = call(
            sum_kernel, shaped((1, width), f32), [spec(pl.ANY)] + [VMEM] * 4, limit=8
        )(crossed, gain_grad, gain_near, gain_mid, gain_far)
        gain_grad = gain_grad + swap(gain_grad, 2)
        column = (kept[b:] + crossed.astype(f32)).astype(bf16)
        more = [beside] + [
            swap(column[k * b : (k + 1) * b], m) for k, m in ((0, 4), (1, 8), (2, 12))
        ]
    else:
        for m in bits_of(count)[1:]:
            gain_grad = gain_grad + swap(gain_grad, m)
        for m in bits_of(count)[1:-1]:
            kept = kept + swap(going, m).astype(f32)
            cut = kept.shape[0] // 2
            kept, going = kept[:cut], kept[cut:].astype(bf16)
        more = [swap(going, count // 2)]
    grad_hidden = call(
        hidden_kernel, shaped((b, width), bf16), [VMEM] * (3 + len(more)), limit=8
    )(backbone_feature_matrix, gain, kept, *more)
    return (grad_hidden, gain_grad[0], scalars[0, 1:2], scalars[0, 0:1])


def solution(mesh):
    in_specs = (
        P(("groups", "vocab"), None),
        P("groups"),
        P("groups", "vocab"),
        P("groups"),
        P(("groups", "vocab")),
        P(("groups", "vocab")),
    )
    out_specs = (P(("groups", "vocab"), None), P("groups"), P("groups"), P("groups"))
    return jax.shard_map(
        on_device, mesh=mesh, in_specs=in_specs, out_specs=out_specs, check_vma=False
    )
```

```python
import functools

import jax
import jax.numpy as jnp
from jax import lax
from jax.experimental import pallas as pl
from jax.experimental.pallas import tpu as pltpu
from jax.sharding import PartitionSpec as P

epsilon = 1e-06
f32 = jnp.float32
bf16 = jnp.bfloat16
LANES = 128
DIGIT_BITS = 7
DIGIT = 1 << DIGIT_BITS
MIB = 1 << 20
STACK_FLOPS = 20 * 10**9
REST_FLOPS = 3 * 10**9
TURN_FLOPS = 3 * 10**9


def cat(*parts):
    return jnp.concatenate(parts, 0)


def bits_of(count):
    return [1 << b for b in range(count.bit_length() - 1)]


class Links:
    def __init__(self, count):
        self.count = count

    def swap(self, value, m):
        return lax.ppermute(value, "vocab", [(i, i ^ m) for i in range(self.count)])

    def gather(self, own, meanwhile):
        swap = self.swap
        if self.count == 16:
            far, near, side = swap(own, 8), swap(own, 4), swap(own, 2)
            across = stack_blocks([near, far], flops=STACK_FLOPS)
            crossed = swap(across, 2)
            beyond, diagonal = swap(side, 12), swap(far, 4)
            result = meanwhile(across)
            chips = stack_blocks([own, side, far, near, beyond, diagonal, crossed], after=result)
            return cat(chips, swap(chips, 1)), result
        blocks, result = own, meanwhile(own)
        for m in reversed(bits_of(self.count)):
            blocks = cat(blocks, swap(blocks, m))
        return blocks, result

    def codes(self):
        if self.count == 16:
            first = [0, 2, 8, 4, 14, 12, 6, 10]
            return first + [c ^ 1 for c in first]
        codes = [0]
        for m in reversed(bits_of(self.count)):
            codes = codes + [c ^ m for c in codes]
        return codes

    def gather_small(self, own, meanwhile):
        swap = self.swap
        result = meanwhile(own)
        if self.count == 16:
            others = [swap(own, m) for m in (4, 8, 12)]
            column = stack_blocks([own] + others, after=result)
            return cat(column, swap(column, 1), swap(column, 2), swap(column, 3)), result
        tiles = own
        for m in bits_of(self.count):
            tiles = cat(tiles, swap(tiles, m))
        return tiles, result

    def small_place(self, code):
        if self.count == 16:
            return (code & 3) * 4 + (code >> 2)
        return code


def spec(space=pltpu.VMEM):
    return pl.BlockSpec(memory_space=space)


SMEM, VMEM, HBM = spec(pltpu.SMEM), spec(), spec(pltpu.HBM)


def call(kernel, outs, ins, scratch=(), flops=0, moved=0, limit=20):
    return pl.pallas_call(
        kernel,
        out_shape=outs,
        in_specs=ins,
        out_specs=jax.tree.map(lambda _: spec(), outs),
        scratch_shapes=list(scratch),
        compiler_params=pltpu.CompilerParams(vmem_limit_bytes=limit * MIB),
        cost_estimate=pl.CostEstimate(flops=flops, bytes_accessed=moved, transcendentals=0),
    )


def shaped(shape, dtype):
    return jax.ShapeDtypeStruct(shape, dtype)


def norm_kernel(ids_hbm, flags_hbm, rows_hbm, gain_hbm, out_ref, ids, flags, rows, gain, sems):
    copies = [
        pltpu.make_async_copy(src, dst, sems.at[k])
        for k, (src, dst) in enumerate(
            [(rows_hbm, rows), (gain_hbm, gain), (ids_hbm, ids), (flags_hbm, flags)]
        )
    ]
    for copy in copies:
        copy.start()
    for copy in copies:
        copy.wait()
    raw = rows[...].astype(f32)
    own_count, width = raw.shape
    inv_rms = lax.rsqrt(jnp.mean(raw * raw, axis=1, keepdims=True) + epsilon)
    out_ref[:, :width] = (raw * inv_rms * gain[...]).astype(bf16)
    row = lax.broadcasted_iota(jnp.int32, (own_count, LANES), 0)
    lane = lax.broadcasted_iota(jnp.int32, (own_count, LANES), 1)
    notes = jnp.zeros((own_count, LANES), jnp.int32)
    for r in range(own_count):
        label = ids[r]
        digits = (
            label & (DIGIT - 1),
            (label >> DIGIT_BITS) & (DIGIT - 1),
            label >> (2 * DIGIT_BITS),
            flags[r],
        )
        for k, digit in enumerate(digits):
            notes = jnp.where((row == r) & (lane == k), digit, notes)
    out_ref[:, width:] = notes.astype(f32).astype(bf16)


def stack_kernel(count, *refs):
    refs[-1][...] = cat(*[ref[...].astype(f32) for ref in refs[:count]]).astype(refs[-1].dtype)


def stack_blocks(blocks, after=None, flops=0):
    rows = sum(block.shape[0] for block in blocks)
    more = [] if after is None else [after]
    return call(
        functools.partial(stack_kernel, len(blocks)),
        shaped((rows, blocks[0].shape[1]), blocks[0].dtype),
        [VMEM] * len(blocks) + [spec(pl.ANY)] * len(more),
        flops=flops,
        limit=8,
    )(*blocks, *more)


def fold(row):
    c = row.shape[1] // 8
    return cat(*[row[:, k * c : (k + 1) * c] for k in range(8)])


def two_parts(value):
    high = value.astype(bf16).astype(f32)
    return jnp.concatenate([high, value - high], 1)


def one_value(parts):
    c = parts.shape[1] // 2
    return parts[:, :c] + parts[:, c:]


def turn_kernel(part, head_ref, order_ref, out_ref):
    step = 512
    width = head_ref.shape[0]
    rows = out_ref.shape[0]

    @pl.loop(0, width // step)
    def _(n):
        here = pl.ds(pl.multiple_of(n * step, step), step)
        out_ref[:, here] = head_ref[here, part * rows : (part + 1) * rows].T


def read_notes(noted):
    label = noted[:, 0:1] + DIGIT * noted[:, 1:2] + DIGIT * DIGIT * noted[:, 2:3]
    return label.astype(jnp.int32), noted[:, 3:4]


def owned_mask(labels, me, slab_width):
    column = lax.broadcasted_iota(jnp.int32, (labels.shape[0], slab_width), 1)
    return column == labels - me * slab_width


def logits_kernel(
    codes, divisor_ref, rows_ref, head_ref, order_ref, scaled_ref, stats_ref, blocks
):
    me = lax.axis_index("vocab")
    width, slab_width = head_ref.shape
    token_count = rows_ref.shape[0]
    own_count = token_count // len(codes)
    scaled_ref[...] = (
        jnp.dot(rows_ref[:, :width], head_ref[...], preferred_element_type=f32) / divisor_ref[0]
    )
    chunk = 128
    for c in range(token_count // chunk):
        band = slice(c * chunk, (c + 1) * chunk)
        scaled = scaled_ref[band, :]
        labels, mask_f = read_notes(rows_ref[band, width:].astype(f32))
        owned = owned_mask(labels, me, slab_width)
        peak = jnp.max(scaled, axis=1, keepdims=True)
        exp_terms = jnp.exp(scaled - peak)
        columns = (
            peak,
            jnp.sum(exp_terms, axis=1, keepdims=True),
            jnp.sum(exp_terms * scaled, axis=1, keepdims=True),
            jnp.sum(jnp.where(owned, scaled, 0.0), axis=1, keepdims=True),
            mask_f,
        )
        lane = lax.broadcasted_iota(jnp.int32, (chunk, LANES), 1)
        tile = jnp.zeros((chunk, LANES), f32)
        for k, column in enumerate(columns):
            tile = jnp.where(lane == k, column, tile)
        for b in range(chunk // own_count):
            owner = me ^ codes[c * (chunk // own_count) + b]
            blocks[owner] = tile[b * own_count : (b + 1) * own_count]
    for c in range(token_count // chunk):
        per = chunk // own_count
        shared = blocks[c * per : (c + 1) * per].reshape(chunk, LANES)
        stats_ref[:, c * chunk : (c + 1) * chunk] = shared.T[:8]


def slab_kernel(
    codes,
    place,
    going_order,
    rest_order,
    divisor_ref,
    tiles_ref,
    rows_ref,
    scaled_ref,
    head_ref,
    head2_ref,
    gain_ref,
    scalars_ref,
    parts_ref,
    kept_ref,
    going_ref,
    rest_ref,
    turned,
    coefs,
):
    me = lax.axis_index("vocab")
    count = len(codes)
    width = head_ref.shape[1]
    cut, slab_width = head_ref.shape[0], 2 * head_ref.shape[0]
    token_count = rows_ref.shape[0]
    own_count = token_count // count
    half = token_count // 2

    def tile(device):
        start = place(device ^ me) * 8
        return tiles_ref[pl.ds(pl.multiple_of(start, 8), 8), :]

    peak = tile(0)[0:1]
    for j in range(1, count):
        peak = jnp.maximum(peak, tile(j)[0:1])
    totals = moments = target_z = jnp.zeros_like(peak)
    for j in range(count):
        t = tile(j)
        fade = jnp.exp(t[0:1] - peak)
        totals += t[1:2] * fade
        moments += t[2:3] * fade
        target_z += t[3:4]
    mask_f = tile(me)[4:5]
    divisor = divisor_ref[0]
    counted = jnp.maximum(jnp.sum(mask_f, axis=1, keepdims=True), 1.0)
    loss = jnp.sum(mask_f * (peak + jnp.log(totals) - target_z), axis=1, keepdims=True) / counted
    temp = -jnp.sum(mask_f * (moments / totals - target_z), axis=1, keepdims=True) / (
        counted * divisor
    )
    lane = lax.broadcasted_iota(jnp.int32, (8, LANES), 1)
    scalars_ref[...] = jnp.where(lane == 0, loss, jnp.where(lane == 1, temp, 0.0))

    factor = mask_f * (token_count / counted) / divisor
    terms = cat(peak, totals, factor, jnp.zeros((LANES - 3, token_count), f32))
    turned[...] = terms.T.reshape(count, own_count, LANES)
    chunk = 64
    per = chunk // own_count
    for c in range(token_count // chunk):
        band = slice(c * chunk, (c + 1) * chunk)
        w = cat(*[turned[me ^ code] for code in codes[c * per : (c + 1) * per]])
        labels, _ = read_notes(rows_ref[band, width:].astype(f32))
        owned = owned_mask(labels, me, slab_width).astype(f32)
        shares = jnp.exp(scaled_ref[band, :] - w[:, 0:1]) / w[:, 1:2]
        coefs[band, :] = (w[:, 2:3] * (shares - owned)).astype(bf16)
    out = jnp.dot(coefs[:, :cut], head_ref[...], preferred_element_type=f32) + jnp.dot(
        coefs[:, cut:], head2_ref[...], preferred_element_type=f32
    )
    kept_ref[...] = out[:half]
    sent = [out[k : k + own_count] for k in range(half, token_count, own_count)]
    going_ref[...] = cat(*[sent[k] for k in going_order]).astype(bf16)
    gain_grad = (
        jnp.sum(out * rows_ref[:, :width].astype(f32), axis=0, keepdims=True) / gain_ref[...]
    )

    parts = two_parts(fold(gain_grad)).astype(bf16)
    parts_ref[...] = parts
    padded = jnp.concatenate(
        [parts.astype(f32), jnp.zeros((8, width - parts.shape[1]), f32)], 1
    )
    rest_ref[...] = cat(*[sent[k] for k in rest_order], padded).astype(bf16)


def pair_kernel(order, at, own_count, kept_ref, twin_ref, *outs):
    twin = twin_ref[...].astype(f32)
    for o, out in zip(order, outs):
        blocks = []
        for k in o:
            t = at.index(k) * own_count
            blocks.append(
                kept_ref[k * own_count : (k + 1) * own_count, :] + twin[t : t + own_count]
            )
        out[...] = cat(*blocks).astype(out.dtype)


def rest_kernel(order, at, own_count, order_ref, kept_ref, twin_ref, parts_ref, gain_out, *outs):
    pair_kernel(order, at, own_count, kept_ref, twin_ref, *outs)
    parts = parts_ref[...].astype(f32)
    twin_parts = twin_ref[...].astype(f32)[twin_ref.shape[0] - 8 :, : parts.shape[1]]
    gain_sum = one_value(parts) + one_value(twin_parts)
    c = gain_out.shape[1] // 8
    for k in range(8):
        gain_out[:, k * c : (k + 1) * c] = gain_sum[k : k + 1, :]


def sum_kernel(order_ref, own_ref, near_ref, mid_ref, far_ref, out_ref):
    out_ref[...] = (own_ref[...] + near_ref[...]) + (mid_ref[...] + far_ref[...])


def hidden_kernel(rows_ref, gain_ref, kept_ref, sum_ref, came_ref, *refs):
    more, (out_ref, gain_out) = refs[:-2], refs[-2:]
    rows = rows_ref[...].astype(f32)
    own_count, width = rows.shape
    inv_rms = lax.rsqrt(jnp.mean(rows * rows, axis=1, keepdims=True) + epsilon)
    units = rows * inv_rms
    grad = kept_ref[:own_count, :]
    for ref in more:
        grad = grad + ref[...].astype(f32)
    grad = grad * gain_ref[...]
    inner_dot = jnp.sum(grad * units, axis=1, keepdims=True)
    out_ref[...] = (inv_rms * (grad - units * inner_dot / width)).astype(bf16)
    gain_out[...] = sum_ref[...] + came_ref[...]


def on_device(
    backbone_feature_matrix,
    closing_rmsnorm_multiplier,
    output_vocab_matrix,
    softness_divisor,
    correct_label_ids,
    included_place_flags,
):
    count = lax.axis_size("vocab")
    links = Links(count)
    swap = links.swap
    codes = links.codes()
    own_count, width = backbone_feature_matrix.shape
    token_count = own_count * count
    half = token_count // 2
    slab_width = output_vocab_matrix.shape[1]
    gain = closing_rmsnorm_multiplier[None, :]
    head_bytes = 2 * width * slab_width
    product = 2 * token_count * width * slab_width

    own = call(
        norm_kernel,
        shaped((own_count, width + LANES), bf16),
        [HBM] * 4,
        [
            pltpu.SMEM((own_count,), jnp.int32),
            pltpu.SMEM((own_count,), jnp.int32),
            pltpu.VMEM((own_count, width), bf16),
            pltpu.VMEM((1, width), f32),
            pltpu.SemaphoreType.DMA((4,)),
        ],
        limit=63,
    )(correct_label_ids, included_place_flags, backbone_feature_matrix, gain)
    def turn(order, part):
        return call(
            functools.partial(turn_kernel, part),
            shaped((slab_width // 2, width), bf16),
            [VMEM, spec(pl.ANY)],
            flops=TURN_FLOPS,
            moved=head_bytes,
            limit=4,
        )(output_vocab_matrix, order)

    rows, left = links.gather(own, lambda order: turn(order, 0))

    scaled, stats = call(
        functools.partial(logits_kernel, codes),
        (shaped((token_count, slab_width), f32), shaped((8, token_count), f32)),
        [SMEM, VMEM, VMEM, spec(pl.ANY)],
        [pltpu.VMEM((count, own_count, LANES), f32)],
        flops=product,
        moved=head_bytes,
    )(softness_divisor, rows, output_vocab_matrix, left)
    tiles, right = links.gather_small(stats, lambda order: turn(order, 1))
    b = own_count
    if count == 16:
        going_order = (6, 7, 4)
        rest_order = ((0, 3, 2, 5), (1,))
        sizes = [(4, f32), (1, bf16)]
    else:
        quarter = count // 4
        going_order = tuple(range(quarter, 2 * quarter))
        rest_order = (tuple(range(quarter)),)
        sizes = [(quarter, f32)]
    rest_at = tuple(sorted(sum(rest_order, ())))

    parts_shape = (8, width // 4)
    scalars, parts, kept, sent_going, sent_rest = call(
        functools.partial(slab_kernel, codes, links.small_place, going_order, rest_at),
        (
            shaped((8, LANES), f32),
            shaped(parts_shape, bf16),
            shaped((half, width), f32),
            shaped((len(going_order) * b, width), bf16),
            shaped((len(rest_at) * b + 8, width), bf16),
        ),
        [SMEM] + [VMEM] * 6,
        [
            pltpu.VMEM((count, own_count, LANES), f32),
            pltpu.VMEM((token_count, slab_width), bf16),
        ],
        flops=product,
        moved=head_bytes,
        limit=28,
    )(softness_divisor, tiles, rows, scaled, left, right, gain)
    twin_going, twin_rest = swap(sent_going, 1), swap(sent_rest, 1)

    going = call(
        functools.partial(pair_kernel, (going_order,), going_order, b),
        shaped((len(going_order) * b, width), bf16),
        [VMEM] * 2,
    )(kept, twin_going)
    gain_grad, kept, *rest = call(
        functools.partial(rest_kernel, rest_order, rest_at, b),
        (shaped((1, width), f32),) + tuple(shaped((k * b, width), t) for k, t in sizes),
        [spec(pl.ANY)] + [VMEM] * 3,
        flops=REST_FLOPS,
    )(going, kept, twin_rest, parts)
    if count == 16:
        crossed = swap(going, 2)
        beside = swap(rest[0], 2)
        gain_far, gain_mid, gain_near = [swap(gain_grad, m) for m in (12, 8, 4)]
        gain_grad = call(
            sum_kernel, shaped((1, width), f32), [spec(pl.ANY)] + [VMEM] * 4, limit=8
        )(crossed, gain_grad, gain_near, gain_mid, gain_far)
        gain_came = swap(gain_grad, 2)
        column = (kept[b:] + crossed.astype(f32)).astype(bf16)
        more = [beside] + [
            swap(column[k * b : (k + 1) * b], m) for k, m in ((0, 4), (1, 8), (2, 12))
        ]
    else:
        for m in bits_of(count)[1:-1]:
            gain_grad = gain_grad + swap(gain_grad, m)
        gain_came = swap(gain_grad, count // 2)
        for m in bits_of(count)[1:-1]:
            kept = kept + swap(going, m).astype(f32)
            cut = kept.shape[0] // 2
            kept, going = kept[:cut], kept[cut:].astype(bf16)
        more = [swap(going, count // 2)]
    grad_hidden, grad_gain = call(
        hidden_kernel,
        (shaped((b, width), bf16), shaped((1, width), f32)),
        [VMEM] * (5 + len(more)),
        limit=8,
    )(backbone_feature_matrix, gain, kept, gain_grad, gain_came, *more)
    return (grad_hidden, grad_gain[0], scalars[0, 1:2], scalars[0, 0:1])


def solution(mesh):
    in_specs = (
        P(("groups", "vocab"), None),
        P("groups"),
        P("groups", "vocab"),
        P("groups"),
        P(("groups", "vocab")),
        P(("groups", "vocab")),
    )
    out_specs = (P(("groups", "vocab"), None), P("groups"), P("groups"), P("groups"))
    return jax.shard_map(
        on_device, mesh=mesh, in_specs=in_specs, out_specs=out_specs, check_vma=False
    )
```
